32 devices in a mesh: sample: 4 (over z), gx: 2 (over core), gy: 2 (over x), gz: 2 (over y).
Axes of the slice: x: 2, y: 2, z: 4, core: 2. Of those that a mesh axis runs over, the one named last changes fastest.
Arguments:
- volume: bfloat16 [16, 32, 32, 128], P(('sample', 'gx'), 'gy', 'gz'), parts along dimension 0, may hold values from -6 to 6
- conv4_weight: bfloat16 [3, 3, 3, 128, 256], replicated, may hold values from -0.109375 to 0.109375
- conv5_weight: bfloat16 [3, 3, 3, 256, 512], P(None, None, None, None, ('gy', 'gz')), may hold values from -0.078125 to 0.078125
Outputs:
- features: bfloat16 [8, 16, 16, 512], P(('sample', 'gx'), None, None, ('gy', 'gz')), parts along dimension 0
The draws below stay inside these ranges and needn't reach their ends.
There are 4 independent parts, one for each index of `sample`. The reference program is written for one: setup_inputs(seed, part) draws one part's arguments, and reference() takes and returns one part's arrays. A program takes and returns all parts, laid end to end along the dimension named above; an argument that names none is the same for every part. Nothing has to cross between parts.
All inputs are finite; a program needn't handle non-finite values.
Results may differ from the reference program's by a relative error of at most 0.009.
Values may be sent and summed in bfloat16 or wider, within the bound.
No kernel may reach another device: no remote copies, remote signals or barrier semaphores. Data moves between devices by JAX's collectives and lax.ppermute only.
A program may use at most 64 MiB of HBM per device.

```python
import jax
import jax.numpy as jnp
from jax import lax

CIN = 128
C4 = 256
C5 = 512
NX = 4
NY = 32
NZ = 32


def levels(rng, extent, cuts, least, top_value):
    loudness, own = 1.0, jax.random.fold_in(rng, 6)
    for axis_at, parts in cuts:
        steps = jnp.exp(jax.random.uniform(jax.random.fold_in(own, axis_at), (parts,), jnp.float32, least / len(cuts), top_value / len(cuts)))
        loudness = loudness * jnp.repeat(steps, extent[axis_at] // parts).reshape([-1 if axis == axis_at else 1 for axis in range(len(extent))])
    return loudness


def scatter_about(stream_key, extent, scale, limit, pieces=(), dtype=jnp.bfloat16):
    gain = levels(stream_key, extent, pieces, -0.22, 0.18) if pieces else 1.0
    entries = jax.random.normal(stream_key, extent, jnp.float32) * scale * gain
    return jnp.minimum(jnp.maximum(entries, -limit), limit).astype(dtype)


def setup_inputs(seed: int = 0, part: int = 0) -> dict:
    seeds = jax.random.split(jax.random.key(seed), 4)
    part_keys = jax.random.split(jax.random.fold_in(seeds[3], part), 4)
    volume = scatter_about(part_keys[0], (NX, NY, NZ, CIN), 1.0, 6.0, ((0, 2), (1, 2), (2, 2)))
    conv4_weight = scatter_about(seeds[1], (3, 3, 3, CIN, C4), (27 * CIN) ** -0.5, 0.109375)
    conv5_weight = scatter_about(seeds[2], (3, 3, 3, C4, C5), (27 * C4) ** -0.5, 0.078125, ((4, 4),))
    return dict(volume=volume, conv4_weight=conv4_weight, conv5_weight=conv5_weight)


def convolve(maps, kernel):
    result = lax.conv_general_dilated(maps.astype(jnp.float32)[None], kernel.astype(jnp.float32), (1, 1, 1), "SAME", dimension_numbers=("NDHWC", "DHWIO", "NDHWC"), precision=lax.Precision.HIGHEST)
    return result[0]


def reference(volume, conv4_weight, conv5_weight):
    hidden = convolve(volume, conv4_weight)
    leaked = jnp.where(hidden > 0, hidden, 0.3 * hidden)
    sizes = leaked.shape
    blocks = leaked.reshape(sizes[0] // 2, 2, sizes[1] // 2, 2, sizes[2] // 2, 2, sizes[3])
    pooled = jnp.max(blocks, axis=(1, 3, 5)).astype(jnp.bfloat16)
    return convolve(pooled, conv5_weight).astype(jnp.bfloat16)
```

```python
import functools

import jax
import jax.numpy as jnp
from jax import lax
from jax.experimental import pallas as pl
from jax.experimental.pallas import tpu as pltpu
from jax.sharding import PartitionSpec as P

BF = jnp.bfloat16
F32 = jnp.float32
VMEM = pl.BlockSpec(memory_space=pltpu.VMEM)
SMEM = pl.BlockSpec(memory_space=pltpu.SMEM)
GROUP = ("gx", "gy", "gz")


def extended(cells, sides, width):
    for axis, dim in sides:
        count = lax.axis_size(axis)
        ends = count - 1
        head = lax.slice_in_dim(cells, 0, width, axis=dim)
        tail = lax.slice_in_dim(cells, cells.shape[dim] - width, cells.shape[dim], axis=dim)
        cells = jnp.concatenate(
            [
                lax.ppermute(tail, axis, [(i, (i + 1) % count) for i in range(ends)]),
                cells,
                lax.ppermute(head, axis, [((i + 1) % count, i) for i in range(ends)]),
            ],
            axis=dim,
        )
    return cells


def conv_local(padded, kernel):
    extent_x = padded.shape[0] - 2
    extent_y = padded.shape[1] - 2
    extent_z = padded.shape[2] - 2
    inputs = padded.shape[3]
    summed = None
    for along_x in range(3):
        for along_y in range(3):
            for along_z in range(3):
                window = padded[
                    along_x : along_x + extent_x,
                    along_y : along_y + extent_y,
                    along_z : along_z + extent_z,
                ]
                window = window.reshape(extent_x * extent_y * extent_z, inputs)
                contrib = jnp.dot(
                    window, kernel[along_x, along_y, along_z], preferred_element_type=jnp.float32
                )
                summed = contrib if summed is None else summed + contrib
    return summed.reshape(extent_x, extent_y, extent_z, kernel.shape[4])


def pool_leaky(hidden):
    leaked = jnp.where(hidden > 0, hidden, 0.3 * hidden)
    sizes = leaked.shape
    blocks = leaked.reshape(sizes[0] // 2, 2, sizes[1] // 2, 2, sizes[2] // 2, 2, sizes[3])
    return jnp.max(blocks, axis=(1, 3, 5)).astype(jnp.bfloat16)


def general_body(volume, conv4_weight, conv5_weight):
    padded = extended(volume, (("gx", 0), ("gy", 1), ("gz", 2)), 1)
    pooled = pool_leaky(conv_local(padded, conv4_weight))
    strips = lax.all_gather(pooled, "gz", axis=2, tiled=True)
    slab = lax.all_gather(strips, "gy", axis=1, tiled=True)
    bordered = extended(slab, (("gx", 0),), 1)
    bordered = jnp.pad(bordered, ((0, 0), (1, 1), (1, 1), (0, 0)))
    return conv_local(bordered, conv5_weight).astype(jnp.bfloat16)


def leaky(v):
    return jnp.where(v > 0, v, 0.3 * v)


def shifted_copies(plane, out_ref, index):
    ny, nz, nc = plane.shape
    flat = plane.reshape(ny * nz, nc).astype(F32)
    at = lax.broadcasted_iota(jnp.int32, flat.shape, 0) % nz
    after = jnp.where(at == 0, 0.0, pltpu.roll(flat, 1, 0))
    before = jnp.where(at == nz - 1, 0.0, pltpu.roll(flat, ny * nz - 1, 0))
    none = jnp.zeros((2, nz, nc), BF)
    for dz, moved in enumerate((after, flat, before)):
        out_ref[dz, index, 0:2] = none
        out_ref[dz, index, 2 + ny : 4 + ny] = none
        out_ref[dz, index, 2 : 2 + ny] = moved.astype(BF).reshape(ny, nz, nc)


def windows(shift_ref, index, first, ny):
    nz, nc = shift_ref.shape[3:]
    parts = []
    for dy in range(3):
        for dz in range(3):
            part = shift_ref[dz, index, pl.ds(first + dy, ny + 1)]
            parts.append(part.reshape((ny + 1) * nz, nc))
    return jnp.concatenate(parts, axis=1)


def edge_windows(plane, flat_ref, col_ref, index, at_y, at_z):
    ny, nz, nc = plane.shape
    flat_ref[index] = plane.reshape(ny * nz, nc).astype(F32)
    low = flat_ref[index, pl.ds(0, ny, nz), :]
    high = flat_ref[index, pl.ds(nz - 1, ny, nz), :]
    col_ref[index] = jnp.zeros(col_ref.shape[1:], F32)
    col_ref[index, 8 : 8 + ny] = jnp.where(at_z == 0, high, low)
    parts = []
    for dy in range(3):
        near = col_ref[index, 7 + dy : 15 + dy + ny]
        far = col_ref[index, 6 + dy : 14 + dy + ny]
        parts.append(jnp.where(at_y == 0, near, far).astype(BF))
    return jnp.concatenate(parts, axis=1)


def edge_weights(w_ref, dx, at_z):
    taps = w_ref.shape[1]
    return jnp.concatenate([w_ref[dx, dy, 2 * at_z] for dy in range(taps)], axis=0)


def own_kernel(at_ref, v_ref, w_ref, h_ref, t_ref, shift_ref, flat_ref, col_ref):
    at_y, at_z = at_ref[1], at_ref[2]
    planes, ny, nz, nc = v_ref.shape
    filters = w_ref.shape[4]
    for p in range(planes):
        shifted_copies(v_ref[p], shift_ref, p)
    wins = [windows(shift_ref, p, 1 - at_y, ny) for p in range(planes)]
    for p in range(planes):
        lhs = jnp.concatenate(wins, axis=1)
        rhs = w_ref[1 - p : 3 - p].reshape(2 * 9 * nc, filters)
        h_ref[p] = jnp.dot(lhs, rhs, preferred_element_type=F32).reshape(h_ref.shape[1:])
    edges = [edge_windows(v_ref[p], flat_ref, col_ref, p, at_y, at_z) for p in range(planes)]
    lhs = jnp.concatenate(edges, axis=1)
    for p in range(planes):
        rhs = jnp.concatenate([edge_weights(w_ref, 1 - p, at_z), edge_weights(w_ref, 2 - p, at_z)], axis=0)
        t_ref[p] = jnp.dot(lhs, rhs, preferred_element_type=F32)


def put(out_ref, first, rows):
    out_ref[first : first + rows.shape[0]] = rows.astype(out_ref.dtype)


def pack_kernel(at_ref, r_ref, w_ref, h_in, t_in, out_ref, h_ref, t_ref, shift_ref, flat_ref, col_ref, pair_ref):
    at_x, at_y, at_z = at_ref[0], at_ref[1], at_ref[2]
    planes, ny, nz, nc = r_ref.shape
    filters = w_ref.shape[4]
    plane = r_ref[at_x]
    dx, mine = 2 * (1 - at_x), 1 - at_x
    shifted_copies(plane, shift_ref, 0)
    lhs = windows(shift_ref, 0, 1 - at_y, ny)
    rhs = w_ref[dx].reshape(9 * nc, filters)
    for p in range(planes):
        h_ref[p * (ny + 1) * nz : (p + 1) * (ny + 1) * nz] = h_in[p].reshape((ny + 1) * nz, filters)
    begin = pl.multiple_of(mine * (ny + 1) * nz, 8)
    h_ref[pl.ds(begin, (ny + 1) * nz)] += jnp.dot(lhs, rhs, preferred_element_type=F32)
    edge = edge_windows(plane, flat_ref, col_ref, 0, at_y, at_z)
    t_ref[...] = t_in[...]
    t_ref[mine] += jnp.dot(edge, edge_weights(w_ref, dx, at_z), preferred_element_type=F32)

    def row(p, e):
        return h_ref[pl.ds(pl.multiple_of((p * (ny + 1) + e) * nz, 8), nz)]

    low = -jnp.inf
    is_edge = lax.broadcasted_iota(jnp.int32, (nz, filters), 0) == (nz - 1) * (1 - at_z)
    for k in range(ny // 2):
        first = jnp.maximum(row(0, at_y + 2 * k), row(1, at_y + 2 * k))
        second = jnp.maximum(row(0, at_y + 2 * k + 1), row(1, at_y + 2 * k + 1))
        if k == 0:
            first = jnp.where(at_y == 1, low, first)
        if k == ny // 2 - 1:
            second = jnp.where(at_y == 0, low, second)
        both = jnp.where(is_edge, low, jnp.maximum(first, second))
        for half in range(filters // 128):
            pair_ref[half, k * nz : (k + 1) * nz] = both[:, half * 128 : (half + 1) * 128]
    pooled = [
        jnp.maximum(
            pair_ref[half, pl.ds(0, ny * nz // 4, 2), :],
            pair_ref[half, pl.ds(1, ny * nz // 4, 2), :],
        )
        for half in range(filters // 128)
    ]
    cells = ny * nz // 4
    put(out_ref, 0, leaky(jnp.concatenate(pooled, axis=1)))
    for p in range(planes):
        put(out_ref, cells + p * nz, row(p, (ny - 1) * (1 - at_y) + at_y))
        put(out_ref, cells + planes * nz + p * nz, row(p, ny * (1 - at_y)))
        base = cells + 2 * planes * nz
        here = p * (ny + 1) * nz
        column = []
        for half in range(filters // 128):
            part = slice(half * 128, (half + 1) * 128)
            flat = pair_ref.at[half]
            for e in range(ny + 1):
                flat[e * nz : (e + 1) * nz] = h_ref[here + e * nz : here + (e + 1) * nz, part]
            picks = [flat[pl.ds(e * nz + z, ny, nz), :] for e in (0, 1) for z in (0, nz - 1)]
            column.append(
                jnp.where(
                    at_y == 0,
                    jnp.where(at_z == 0, picks[1], picks[0]),
                    jnp.where(at_z == 0, picks[3], picks[2]),
                )
            )
        put(out_ref, base + p * ny, jnp.concatenate(column, axis=1))
        base += planes * ny
        put(out_ref, base + p * ny, jnp.where(at_y == 0, t_ref[p, 0:ny], t_ref[p, 1 : ny + 1]))
    base += planes * ny
    corner = jnp.where(at_y == 0, t_ref[:, ny : ny + 1], t_ref[:, 0:1])
    at = lax.broadcasted_iota(jnp.int32, (16, filters), 0)
    put(out_ref, base, jnp.where(at == 0, corner[0], jnp.where(at == 1, corner[1], 0.0)))


def finish_kernel(at_ref, q0, q1, q2, q3, w_ref, own_ref, other_ref, pack_ref, full_ref, pair_ref, shift_ref, *, ny, nz, planes):
    at_x, at_y, at_z = at_ref[0], at_ref[1], at_ref[2]
    filters = w_ref.shape[3]
    outs = w_ref.shape[4]
    here = 2 * at_y + at_z
    pack_ref[here] = q0[...]
    pack_ref[2 * (1 - at_y) + at_z] = q1[...]
    pack_ref[2 * at_y + 1 - at_z] = q2[...]
    pack_ref[2 * (1 - at_y) + 1 - at_z] = q3[...]
    py, pz = ny // 2, nz // 2
    cells = py * pz
    row_at = cells
    over_y = row_at + planes * nz
    col_at = over_y + planes * nz
    over_z = col_at + planes * ny
    over_c = over_z + planes * ny

    def take(q, first, count):
        return pack_ref[q, first : first + count].astype(F32)

    def halve(v, slot):
        parts = []
        for half in range(filters // 128):
            pair_ref[slot, half] = v[:, half * 128 : (half + 1) * 128]
            count = v.shape[0] // 2
            parts.append(
                jnp.maximum(pair_ref[slot, half, pl.ds(0, count, 2), :], pair_ref[slot, half, pl.ds(1, count, 2), :])
            )
        return jnp.concatenate(parts, axis=1)

    for qy in range(2):
        for qz in range(2):
            q, by_y, by_z, by_both = 2 * qy + qz, 2 * (1 - qy) + qz, 2 * qy + 1 - qz, 2 * (1 - qy) + 1 - qz
            y_edge, z_edge = (ny - 1) * (1 - qy), (nz - 1) * (1 - qz)
            corner = take(by_both, over_c, 16)
            edge_row, edge_col = None, None
            at = lax.broadcasted_iota(jnp.int32, (nz, filters), 0)
            for p in range(planes):
                across = take(by_z, over_z + p * ny, ny)
                extra = across[y_edge : y_edge + 1] + corner[p : p + 1]
                line = take(q, row_at + p * nz, nz) + take(by_y, over_y + p * nz, nz)
                line = jnp.where(at == z_edge, line + extra, line)
                edge_row = line if edge_row is None else jnp.maximum(edge_row, line)
                line = take(q, col_at + p * ny, ny) + across
                edge_col = line if edge_col is None else jnp.maximum(edge_col, line)
            edge_col = jnp.where(at == y_edge, -jnp.inf, edge_col)
            edge_row = leaky(halve(edge_row, 0))
            edge_col = leaky(halve(edge_col, 1))
            pooled = take(q, 0, cells).reshape(py, pz, filters)
            inner = lax.broadcasted_iota(jnp.int32, (py, pz, filters), 1) == (pz - 1) * (1 - qz)
            pooled = jnp.where(inner, jnp.maximum(pooled, edge_col[:, None, :]), pooled)
            inner = lax.broadcasted_iota(jnp.int32, (py, pz, filters), 0) == (py - 1) * (1 - qy)
            pooled = jnp.where(inner, jnp.maximum(pooled, edge_row[None]), pooled)
            full_ref[qy * py : (qy + 1) * py, qz * pz : (qz + 1) * pz] = pooled
    shifted_copies(full_ref[...].astype(BF), shift_ref, 0)
    parts = []
    for dy in range(3):
        for dz in range(3):
            parts.append(shift_ref[dz, 0, 1 + dy : 1 + dy + ny].reshape(ny * nz, filters))
    lhs = jnp.concatenate(parts, axis=1)
    rhs = jnp.concatenate(
        [w_ref[1].reshape(9 * filters, outs), w_ref[2 * at_x].reshape(9 * filters, outs)], axis=1
    )
    sums = jnp.dot(lhs, rhs, preferred_element_type=F32)
    own_ref[...] = sums[:, :outs]
    other_ref[...] = sums[:, outs:]


def pair_body(volume, conv4_weight, conv5_weight):
    planes, ny, nz, nc = volume.shape
    f4, f5 = conv4_weight.shape[4], conv5_weight.shape[4]
    at = jnp.stack([lax.axis_index(axis) for axis in GROUP]).astype(jnp.int32)

    def swap(x, flips):
        return lax.ppermute(x, GROUP, [(i, i ^ flips) for i in range(8)])

    cost = functools.partial(pl.CostEstimate, transcendentals=0)
    rows = (ny + 1) * nz
    theirs = swap(volume, 4)
    hidden, past = pl.pallas_call(
        own_kernel,
        out_shape=(
            jax.ShapeDtypeStruct((planes, ny + 1, nz, f4), F32),
            jax.ShapeDtypeStruct((planes, ny + 8, f4), F32),
        ),
        in_specs=[SMEM, VMEM, VMEM],
        out_specs=(VMEM, VMEM),
        scratch_shapes=[
            pltpu.VMEM((3, planes, ny + 4, nz, nc), BF),
            pltpu.VMEM((planes, ny * nz, nc), F32),
            pltpu.VMEM((planes, ny + 24, nc), F32),
        ],
        cost_estimate=cost(flops=2 * planes * rows * 18 * nc * f4, bytes_accessed=54 * nc * f4),
        name="own_planes",
    )(at, volume, conv4_weight)
    cells = ny * nz // 4
    packed = cells + planes * (2 * nz + 2 * ny) + 16
    pack = pl.pallas_call(
        pack_kernel,
        out_shape=jax.ShapeDtypeStruct((packed, f4), BF),
        in_specs=[SMEM, VMEM, VMEM, VMEM, VMEM],
        out_specs=VMEM,
        scratch_shapes=[
            pltpu.VMEM((planes * rows, f4), F32),
            pltpu.VMEM((planes, ny + 8, f4), F32),
            pltpu.VMEM((3, 1, ny + 4, nz, nc), BF),
            pltpu.VMEM((1, ny * nz, nc), F32),
            pltpu.VMEM((1, ny + 24, nc), F32),
            pltpu.VMEM((f4 // 128, rows, 128), F32),
        ],
        cost_estimate=cost(flops=2 * rows * 9 * nc * f4, bytes_accessed=18 * nc * f4),
        name="pool_and_pack",
    )(at, theirs, conv4_weight, hidden, past)
    by_y = swap(pack, 2)
    by_z = swap(pack, 1)
    by_both = swap(pack, 3)
    gy, gz = 2 * ny // 2, 2 * nz // 2
    own, other = pl.pallas_call(
        functools.partial(finish_kernel, ny=ny, nz=nz, planes=planes),
        out_shape=(jax.ShapeDtypeStruct((gy * gz, f5), F32), jax.ShapeDtypeStruct((gy * gz, f5), F32)),
        in_specs=[SMEM] + [VMEM] * 5,
        out_specs=(VMEM, VMEM),
        scratch_shapes=[
            pltpu.VMEM((4, packed, f4), BF),
            pltpu.VMEM((gy, gz, f4), F32),
            pltpu.VMEM((2, f4 // 128, max(ny, nz), 128), F32),
            pltpu.VMEM((3, 1, gy + 4, gz, f4), BF),
        ],
        cost_estimate=cost(flops=4 * gy * gz * 9 * f4 * f5, bytes_accessed=36 * f4 * f5),
        name="finish_and_conv5",
    )(at, pack, by_y, by_z, by_both, conv5_weight)
    features = (own + swap(other, 4)).astype(BF)
    return features.reshape(1, gy, gz, f5)


def body(volume, conv4_weight, conv5_weight):
    if all(lax.axis_size(axis) == 2 for axis in GROUP) and volume.shape[0] == 2:
        return pair_body(volume, conv4_weight, conv5_weight)
    return general_body(volume, conv4_weight, conv5_weight)


def solution(mesh):
    return jax.shard_map(
        body,
        mesh=mesh,
        in_specs=(
            P(("sample", "gx"), "gy", "gz", None),
            P(),
            P(None, None, None, None, ("gy", "gz")),
        ),
        out_specs=P(("sample", "gx"), None, None, ("gy", "gz")),
        check_vma=False,
    )
```

```python
import functools

import jax
import jax.numpy as jnp
from jax import lax
from jax.experimental import pallas as pl
from jax.experimental.pallas import tpu as pltpu
from jax.sharding import PartitionSpec as P

BF = jnp.bfloat16
F32 = jnp.float32
VMEM = pl.BlockSpec(memory_space=pltpu.VMEM)
HBM = pl.BlockSpec(memory_space=pltpu.HBM)
GROUP = ("gx", "gy", "gz")
PARAMS = pltpu.CompilerParams(vmem_limit_bytes=8 * 2**20)


def extended(cells, sides, width):
    for axis, dim in sides:
        count = lax.axis_size(axis)
        ends = count - 1
        head = lax.slice_in_dim(cells, 0, width, axis=dim)
        tail = lax.slice_in_dim(cells, cells.shape[dim] - width, cells.shape[dim], axis=dim)
        cells = jnp.concatenate(
            [
                lax.ppermute(tail, axis, [(i, (i + 1) % count) for i in range(ends)]),
                cells,
                lax.ppermute(head, axis, [((i + 1) % count, i) for i in range(ends)]),
            ],
            axis=dim,
        )
    return cells


def conv_local(padded, kernel):
    extent_x = padded.shape[0] - 2
    extent_y = padded.shape[1] - 2
    extent_z = padded.shape[2] - 2
    inputs = padded.shape[3]
    summed = None
    for along_x in range(3):
        for along_y in range(3):
            for along_z in range(3):
                window = padded[
                    along_x : along_x + extent_x,
                    along_y : along_y + extent_y,
                    along_z : along_z + extent_z,
                ]
                window = window.reshape(extent_x * extent_y * extent_z, inputs)
                contrib = jnp.dot(
                    window, kernel[along_x, along_y, along_z], preferred_element_type=jnp.float32
                )
                summed = contrib if summed is None else summed + contrib
    return summed.reshape(extent_x, extent_y, extent_z, kernel.shape[4])


def pool_leaky(hidden):
    leaked = jnp.where(hidden > 0, hidden, 0.3 * hidden)
    sizes = leaked.shape
    blocks = leaked.reshape(sizes[0] // 2, 2, sizes[1] // 2, 2, sizes[2] // 2, 2, sizes[3])
    return jnp.max(blocks, axis=(1, 3, 5)).astype(jnp.bfloat16)


def general_body(volume, conv4_weight, conv5_weight):
    padded = extended(volume, (("gx", 0), ("gy", 1), ("gz", 2)), 1)
    pooled = pool_leaky(conv_local(padded, conv4_weight))
    strips = lax.all_gather(pooled, "gz", axis=2, tiled=True)
    slab = lax.all_gather(strips, "gy", axis=1, tiled=True)
    bordered = extended(slab, (("gx", 0),), 1)
    bordered = jnp.pad(bordered, ((0, 0), (1, 1), (1, 1), (0, 0)))
    return conv_local(bordered, conv5_weight).astype(jnp.bfloat16)


def leaky(v):
    return jnp.where(v > 0, v, 0.3 * v)


def shifted_copies(plane, out_ref, index):
    ny, nz, nc = plane.shape
    flat = plane.reshape(ny * nz, nc).astype(F32)
    at = lax.broadcasted_iota(jnp.int32, flat.shape, 0) % nz
    after = jnp.where(at == 0, 0.0, pltpu.roll(flat, 1, 0))
    before = jnp.where(at == nz - 1, 0.0, pltpu.roll(flat, ny * nz - 1, 0))
    none = jnp.zeros((2, nz, nc), BF)
    for dz, moved in enumerate((after, flat, before)):
        out_ref[dz, index, 0:2] = none
        out_ref[dz, index, 2 + ny : 4 + ny] = none
        out_ref[dz, index, 2 : 2 + ny] = moved.astype(BF).reshape(ny, nz, nc)


def windows(shift_ref, index, first, ny):
    nz, nc = shift_ref.shape[3:]
    parts = []
    for dy in range(3):
        for dz in range(3):
            part = shift_ref[dz, index, pl.ds(first + dy, ny + 1)]
            parts.append(part.reshape((ny + 1) * nz, nc))
    return jnp.concatenate(parts, axis=1)


def edge_windows(plane, flat_ref, col_ref, index, at_y, at_z):
    ny, nz, nc = plane.shape
    flat_ref[index] = plane.reshape(ny * nz, nc).astype(F32)
    low = flat_ref[index, pl.ds(0, ny, nz), :]
    high = flat_ref[index, pl.ds(nz - 1, ny, nz), :]
    col_ref[index] = jnp.zeros(col_ref.shape[1:], F32)
    col_ref[index, 8 : 8 + ny] = jnp.where(at_z == 0, high, low)
    parts = []
    for dy in range(3):
        near = col_ref[index, 7 + dy : 15 + dy + ny]
        far = col_ref[index, 6 + dy : 14 + dy + ny]
        parts.append(jnp.where(at_y == 0, near, far).astype(BF))
    return jnp.concatenate(parts, axis=1)


def edge_weights(w_ref, dx, at_z):
    taps = w_ref.shape[1]
    return jnp.concatenate([w_ref[dx, dy, 2 * at_z] for dy in range(taps)], axis=0)


def own_kernel(v_hbm, w_hbm, h_ref, t_ref, w_ref, v_ref, shift_ref, flat_ref, col_ref, w_sem, v_sem):
    load = pltpu.make_async_copy(v_hbm, v_ref, v_sem)
    load.start()
    order = (1, 0, 2)
    loads = {dx: pltpu.make_async_copy(w_hbm.at[dx], w_ref.at[dx], w_sem.at[dx]) for dx in order}
    for dx in order:
        loads[dx].start()
    at_y, at_z = lax.axis_index("gy"), lax.axis_index("gz")
    planes, ny, nz, nc = v_ref.shape
    filters = w_ref.shape[4]
    load.wait()
    for p in range(planes):
        shifted_copies(v_ref[p], shift_ref, p)
    wins = [windows(shift_ref, p, 1 - at_y, ny) for p in range(planes)]
    edges = [edge_windows(v_ref[p], flat_ref, col_ref, p, at_y, at_z) for p in range(planes)]
    for dx in order:
        loads[dx].wait()
        for p in range(planes):
            source = p + dx - 1
            if not 0 <= source < planes:
                continue
            rhs = w_ref[dx].reshape(9 * nc, filters)
            sums = jnp.dot(wins[source], rhs, preferred_element_type=F32).reshape(h_ref.shape[1:])
            past = jnp.dot(edges[source], edge_weights(w_ref, dx, at_z), preferred_element_type=F32)
            if dx == order[0]:
                h_ref[p] = sums
                t_ref[p] = past
            else:
                h_ref[p] += sums
                t_ref[p] += past


def put(out_ref, first, rows):
    out_ref[first : first + rows.shape[0]] = rows.astype(out_ref.dtype)


def pack_kernel(r_ref, w_ref, h_in, t_in, out_ref, h_ref, t_ref, shift_ref, flat_ref, col_ref, pair_ref):
    at_x, at_y, at_z = (lax.axis_index(axis) for axis in GROUP)
    planes, ny, nz, nc = r_ref.shape
    filters = w_ref.shape[4]
    plane = r_ref[at_x]
    dx, mine = 2 * (1 - at_x), 1 - at_x
    shifted_copies(plane, shift_ref, 0)
    lhs = windows(shift_ref, 0, 1 - at_y, ny)
    rhs = w_ref[dx].reshape(9 * nc, filters)
    for p in range(planes):
        h_ref[p * (ny + 1) * nz : (p + 1) * (ny + 1) * nz] = h_in[p].reshape((ny + 1) * nz, filters)
    begin = pl.multiple_of(mine * (ny + 1) * nz, 8)
    h_ref[pl.ds(begin, (ny + 1) * nz)] += jnp.dot(lhs, rhs, preferred_element_type=F32)
    edge = edge_windows(plane, flat_ref, col_ref, 0, at_y, at_z)
    t_ref[...] = t_in[...]
    t_ref[mine] += jnp.dot(edge, edge_weights(w_ref, dx, at_z), preferred_element_type=F32)

    def row(p, e):
        return h_ref[pl.ds(pl.multiple_of((p * (ny + 1) + e) * nz, 8), nz)]

    low = -jnp.inf
    y_edge = lax.broadcasted_iota(jnp.int32, (ny, filters), 0) == (ny - 1) * (1 - at_y)
    is_edge = lax.broadcasted_iota(jnp.int32, (nz, filters), 0) == (nz - 1) * (1 - at_z)
    for k in range(ny // 2):
        first = jnp.maximum(row(0, at_y + 2 * k), row(1, at_y + 2 * k))
        second = jnp.maximum(row(0, at_y + 2 * k + 1), row(1, at_y + 2 * k + 1))
        if k == 0:
            first = jnp.where(at_y == 1, low, first)
        if k == ny // 2 - 1:
            second = jnp.where(at_y == 0, low, second)
        both = jnp.where(is_edge, low, jnp.maximum(first, second))
        for half in range(filters // 128):
            pair_ref[half, k * nz : (k + 1) * nz] = both[:, half * 128 : (half + 1) * 128]
    pooled = [
        jnp.maximum(
            pair_ref[half, pl.ds(0, ny * nz // 4, 2), :],
            pair_ref[half, pl.ds(1, ny * nz // 4, 2), :],
        )
        for half in range(filters // 128)
    ]
    cells = ny * nz // 4
    put(out_ref, 0, leaky(jnp.concatenate(pooled, axis=1)))
    for p in range(planes):
        put(out_ref, cells + p * nz, row(p, (ny - 1) * (1 - at_y) + at_y))
        put(out_ref, cells + planes * nz + p * nz, row(p, ny * (1 - at_y)))
        base = cells + 2 * planes * nz
        here = p * (ny + 1) * nz
        column = []
        for half in range(filters // 128):
            part = slice(half * 128, (half + 1) * 128)
            flat = pair_ref.at[half]
            for e in range(ny + 1):
                flat[e * nz : (e + 1) * nz] = h_ref[here + e * nz : here + (e + 1) * nz, part]
            picks = [flat[pl.ds(e * nz + z, ny, nz), :] for e in (0, 1) for z in (0, nz - 1)]
            column.append(
                jnp.where(
                    at_y == 0,
                    jnp.where(at_z == 0, picks[1], picks[0]),
                    jnp.where(at_z == 0, picks[3], picks[2]),
                )
            )
        corner = jnp.where(at_y == 0, t_ref[p, ny : ny + 1], t_ref[p, 0:1])
        column = jnp.where(y_edge, corner, jnp.concatenate(column, axis=1))
        put(out_ref, base + p * ny, column)
        base += planes * ny
        put(out_ref, base + p * ny, jnp.where(at_y == 0, t_ref[p, 0:ny], t_ref[p, 1 : ny + 1]))


def finish_kernel(q0, q1, q2, q3, w_ref, own_ref, other_ref, pack_ref, full_ref, pair_ref, shift_ref, *, ny, nz, planes):
    at_x, at_y, at_z = (lax.axis_index(axis) for axis in GROUP)
    filters = w_ref.shape[3]
    outs = w_ref.shape[4]
    here = 2 * at_y + at_z
    pack_ref[here] = q0[...]
    pack_ref[2 * (1 - at_y) + at_z] = q1[...]
    pack_ref[2 * at_y + 1 - at_z] = q2[...]
    pack_ref[2 * (1 - at_y) + 1 - at_z] = q3[...]
    py, pz = ny // 2, nz // 2
    cells = py * pz
    row_at = cells
    over_y = row_at + planes * nz
    col_at = over_y + planes * nz
    over_z = col_at + planes * ny

    def take(q, first, count):
        return pack_ref[q, first : first + count].astype(F32)

    def halve(v, slot):
        parts = []
        for half in range(filters // 128):
            pair_ref[slot, half] = v[:, half * 128 : (half + 1) * 128]
            count = v.shape[0] // 2
            parts.append(
                jnp.maximum(pair_ref[slot, half, pl.ds(0, count, 2), :], pair_ref[slot, half, pl.ds(1, count, 2), :])
            )
        return jnp.concatenate(parts, axis=1)

    for qy in range(2):
        for qz in range(2):
            q, by_y, by_z, by_both = 2 * qy + qz, 2 * (1 - qy) + qz, 2 * qy + 1 - qz, 2 * (1 - qy) + 1 - qz
            y_edge, z_edge = (ny - 1) * (1 - qy), (nz - 1) * (1 - qz)
            edge_row, edge_col = None, None
            at = lax.broadcasted_iota(jnp.int32, (nz, filters), 0)
            for p in range(planes):
                across = take(by_z, over_z + p * ny, ny)
                corner = take(by_both, col_at + p * ny, ny)[ny - 1 - y_edge : ny - y_edge]
                extra = across[y_edge : y_edge + 1] + corner
                line = take(q, row_at + p * nz, nz) + take(by_y, over_y + p * nz, nz)
                line = jnp.where(at == z_edge, line + extra, line)
                edge_row = line if edge_row is None else jnp.maximum(edge_row, line)
                line = take(q, col_at + p * ny, ny) + across
                edge_col = line if edge_col is None else jnp.maximum(edge_col, line)
            edge_col = jnp.where(at == y_edge, -jnp.inf, edge_col)
            edge_row = leaky(halve(edge_row, 0))
            edge_col = leaky(halve(edge_col, 1))
            pooled = take(q, 0, cells).reshape(py, pz, filters)
            inner = lax.broadcasted_iota(jnp.int32, (py, pz, filters), 1) == (pz - 1) * (1 - qz)
            pooled = jnp.where(inner, jnp.maximum(pooled, edge_col[:, None, :]), pooled)
            inner = lax.broadcasted_iota(jnp.int32, (py, pz, filters), 0) == (py - 1) * (1 - qy)
            pooled = jnp.where(inner, jnp.maximum(pooled, edge_row[None]), pooled)
            full_ref[qy * py : (qy + 1) * py, qz * pz : (qz + 1) * pz] = pooled
    shifted_copies(full_ref[...].astype(BF), shift_ref, 0)
    parts = []
    for dy in range(3):
        for dz in range(3):
            parts.append(shift_ref[dz, 0, 1 + dy : 1 + dy + ny].reshape(ny * nz, filters))
    lhs = jnp.concatenate(parts, axis=1)
    rhs = jnp.concatenate(
        [w_ref[1].reshape(9 * filters, outs), w_ref[2 * at_x].reshape(9 * filters, outs)], axis=1
    )
    sums = jnp.dot(lhs, rhs, preferred_element_type=F32)
    own_ref[...] = sums[:, :outs]
    other_ref[...] = sums[:, outs:]


def add_kernel(own_ref, other_ref, out_ref):
    out_ref[...] = (own_ref[...] + other_ref[...]).astype(out_ref.dtype)


def pair_body(volume, conv4_weight, conv5_weight):
    planes, ny, nz, nc = volume.shape
    f4, f5 = conv4_weight.shape[4], conv5_weight.shape[4]

    def swap(x, flips):
        return lax.ppermute(x, GROUP, [(i, i ^ flips) for i in range(8)])

    cost = functools.partial(pl.CostEstimate, transcendentals=0)
    rows = (ny + 1) * nz
    theirs = swap(volume, 4)
    hidden, past, kernel4 = pl.pallas_call(
        own_kernel,
        out_shape=(
            jax.ShapeDtypeStruct((planes, ny + 1, nz, f4), F32),
            jax.ShapeDtypeStruct((planes, ny + 8, f4), F32),
            jax.ShapeDtypeStruct(conv4_weight.shape, BF),
        ),
        in_specs=[HBM, HBM],
        out_specs=(VMEM, VMEM, VMEM),
        scratch_shapes=[
            pltpu.VMEM(volume.shape, BF),
            pltpu.VMEM((3, planes, ny + 4, nz, nc), BF),
            pltpu.VMEM((planes, ny * nz, nc), F32),
            pltpu.VMEM((planes, ny + 24, nc), F32),
            pltpu.SemaphoreType.DMA((3,)),
            pltpu.SemaphoreType.DMA,
        ],
        cost_estimate=cost(flops=2 * planes * rows * 18 * nc * f4, bytes_accessed=54 * nc * f4),
        compiler_params=PARAMS,
        name="own_planes",
    )(*(pltpu.with_memory_space_constraint(x, pltpu.HBM) for x in (volume, conv4_weight)))
    cells = ny * nz // 4
    packed = cells + planes * (2 * nz + 2 * ny)
    pack = pl.pallas_call(
        pack_kernel,
        out_shape=jax.ShapeDtypeStruct((packed, f4), BF),
        in_specs=[VMEM] * 4,
        out_specs=VMEM,
        scratch_shapes=[
            pltpu.VMEM((planes * rows, f4), F32),
            pltpu.VMEM((planes, ny + 8, f4), F32),
            pltpu.VMEM((3, 1, ny + 4, nz, nc), BF),
            pltpu.VMEM((1, ny * nz, nc), F32),
            pltpu.VMEM((1, ny + 24, nc), F32),
            pltpu.VMEM((f4 // 128, rows, 128), F32),
        ],
        cost_estimate=cost(flops=2 * rows * 9 * nc * f4, bytes_accessed=18 * nc * f4),
        compiler_params=PARAMS,
        name="pool_and_pack",
    )(theirs, kernel4, hidden, past)
    by_y = swap(pack, 2)
    by_z = swap(pack, 1)
    by_both = swap(pack, 3)
    gy, gz = 2 * ny // 2, 2 * nz // 2
    own, other = pl.pallas_call(
        functools.partial(finish_kernel, ny=ny, nz=nz, planes=planes),
        out_shape=(jax.ShapeDtypeStruct((gy * gz, f5), F32), jax.ShapeDtypeStruct((gy * gz, f5), F32)),
        in_specs=[VMEM] * 5,
        out_specs=(VMEM, VMEM),
        scratch_shapes=[
            pltpu.VMEM((4, packed, f4), BF),
            pltpu.VMEM((gy, gz, f4), F32),
            pltpu.VMEM((2, f4 // 128, max(ny, nz), 128), F32),
            pltpu.VMEM((3, 1, gy + 4, gz, f4), BF),
        ],
        cost_estimate=cost(flops=4 * gy * gz * 9 * f4 * f5, bytes_accessed=36 * f4 * f5),
        compiler_params=PARAMS,
        name="finish_and_conv5",
    )(pack, by_y, by_z, by_both, conv5_weight)
    features = pl.pallas_call(
        add_kernel,
        out_shape=jax.ShapeDtypeStruct((gy * gz, f5), BF),
        in_specs=[VMEM] * 2,
        out_specs=VMEM,
        compiler_params=PARAMS,
        name="add_planes",
    )(own, swap(other, 4))
    return features.reshape(1, gy, gz, f5)


def body(volume, conv4_weight, conv5_weight):
    if all(lax.axis_size(axis) == 2 for axis in GROUP) and volume.shape[0] == 2:
        return pair_body(volume, conv4_weight, conv5_weight)
    return general_body(volume, conv4_weight, conv5_weight)


def solution(mesh):
    return jax.shard_map(
        body,
        mesh=mesh,
        in_specs=(
            P(("sample", "gx"), "gy", "gz", None),
            P(),
            P(None, None, None, None, ("gy", "gz")),
        ),
        out_specs=P(("sample", "gx"), None, None, ("gy", "gz")),
        check_vma=False,
    )
```

```python
import functools

import jax
import jax.numpy as jnp
from jax import lax
from jax.experimental import pallas as pl
from jax.experimental.pallas import tpu as pltpu
from jax.sharding import PartitionSpec as P

BF = jnp.bfloat16
F32 = jnp.float32
VMEM = pl.BlockSpec(memory_space=pltpu.VMEM)
HBM = pl.BlockSpec(memory_space=pltpu.HBM)
GROUP = ("gx", "gy", "gz")
PARAMS = pltpu.CompilerParams(vmem_limit_bytes=8 * 2**20)


def extended(cells, sides, width):
    for axis, dim in sides:
        count = lax.axis_size(axis)
        ends = count - 1
        head = lax.slice_in_dim(cells, 0, width, axis=dim)
        tail = lax.slice_in_dim(cells, cells.shape[dim] - width, cells.shape[dim], axis=dim)
        cells = jnp.concatenate(
            [
                lax.ppermute(tail, axis, [(i, (i + 1) % count) for i in range(ends)]),
                cells,
                lax.ppermute(head, axis, [((i + 1) % count, i) for i in range(ends)]),
            ],
            axis=dim,
        )
    return cells


def conv_local(padded, kernel):
    extent_x = padded.shape[0] - 2
    extent_y = padded.shape[1] - 2
    extent_z = padded.shape[2] - 2
    inputs = padded.shape[3]
    summed = None
    for along_x in range(3):
        for along_y in range(3):
            for along_z in range(3):
                window = padded[
                    along_x : along_x + extent_x,
                    along_y : along_y + extent_y,
                    along_z : along_z + extent_z,
                ]
                window = window.reshape(extent_x * extent_y * extent_z, inputs)
                contrib = jnp.dot(
                    window, kernel[along_x, along_y, along_z], preferred_element_type=jnp.float32
                )
                summed = contrib if summed is None else summed + contrib
    return summed.reshape(extent_x, extent_y, extent_z, kernel.shape[4])


def pool_leaky(hidden):
    leaked = jnp.where(hidden > 0, hidden, 0.3 * hidden)
    sizes = leaked.shape
    blocks = leaked.reshape(sizes[0] // 2, 2, sizes[1] // 2, 2, sizes[2] // 2, 2, sizes[3])
    return jnp.max(blocks, axis=(1, 3, 5)).astype(jnp.bfloat16)


def general_body(volume, conv4_weight, conv5_weight):
    padded = extended(volume, (("gx", 0), ("gy", 1), ("gz", 2)), 1)
    pooled = pool_leaky(conv_local(padded, conv4_weight))
    strips = lax.all_gather(pooled, "gz", axis=2, tiled=True)
    slab = lax.all_gather(strips, "gy", axis=1, tiled=True)
    bordered = extended(slab, (("gx", 0),), 1)
    bordered = jnp.pad(bordered, ((0, 0), (1, 1), (1, 1), (0, 0)))
    return conv_local(bordered, conv5_weight).astype(jnp.bfloat16)


def leaky(v):
    return jnp.where(v > 0, v, 0.3 * v)


def shifted_copies(plane, out_ref, index):
    ny, nz, nc = plane.shape
    flat = plane.reshape(ny * nz, nc).astype(F32)
    at = lax.broadcasted_iota(jnp.int32, flat.shape, 0) % nz
    after = jnp.where(at == 0, 0.0, pltpu.roll(flat, 1, 0))
    before = jnp.where(at == nz - 1, 0.0, pltpu.roll(flat, ny * nz - 1, 0))
    none = jnp.zeros((2, nz, nc), BF)
    for dz, moved in enumerate((after, flat, before)):
        out_ref[dz, index, 0:2] = none
        out_ref[dz, index, 2 + ny : 4 + ny] = none
        out_ref[dz, index, 2 : 2 + ny] = moved.astype(BF).reshape(ny, nz, nc)


def windows(shift_ref, index, first, ny):
    nz, nc = shift_ref.shape[3:]
    parts = []
    for dy in range(3):
        for dz in range(3):
            part = shift_ref[dz, index, pl.ds(first + dy, ny + 1)]
            parts.append(part.reshape((ny + 1) * nz, nc))
    return jnp.concatenate(parts, axis=1)


def edge_windows(plane, flat_ref, col_ref, index, at_y, at_z):
    ny, nz, nc = plane.shape
    flat_ref[index] = plane.reshape(ny * nz, nc).astype(F32)
    low = flat_ref[index, pl.ds(0, ny, nz), :]
    high = flat_ref[index, pl.ds(nz - 1, ny, nz), :]
    col_ref[index] = jnp.zeros(col_ref.shape[1:], F32)
    col_ref[index, 8 : 8 + ny] = jnp.where(at_z == 0, high, low)
    parts = []
    for dy in range(3):
        near = col_ref[index, 7 + dy : 15 + dy + ny]
        far = col_ref[index, 6 + dy : 14 + dy + ny]
        parts.append(jnp.where(at_y == 0, near, far).astype(BF))
    return jnp.concatenate(parts, axis=1)


def edge_weights(w_ref, dx, at_z):
    taps = w_ref.shape[1]
    return jnp.concatenate([w_ref[dx, dy, 2 * at_z] for dy in range(taps)], axis=0)


def prepare_kernel(v_hbm, w_hbm, shift_ref, edge_ref, w_ref, v_ref, flat_ref, col_ref, v_sem, w_sem):
    load_v = pltpu.make_async_copy(v_hbm, v_ref, v_sem)
    load_w = pltpu.make_async_copy(w_hbm, w_ref, w_sem)
    load_v.start()
    load_w.start()
    at_y, at_z = lax.axis_index("gy"), lax.axis_index("gz")
    load_v.wait()
    for p in range(v_ref.shape[0]):
        shifted_copies(v_ref[p], shift_ref, p)
        edge_ref[p] = edge_windows(v_ref[p], flat_ref, col_ref, p, at_y, at_z)
    load_w.wait()


def put(out_ref, first, rows):
    out_ref[first : first + rows.shape[0]] = rows.astype(out_ref.dtype)


def pack_kernel(r_ref, w_ref, own_ref, edge_ref, out_ref, h_ref, t_ref, shift_ref, flat_ref, col_ref, pair_ref):
    at_x, at_y, at_z = (lax.axis_index(axis) for axis in GROUP)
    planes, ny, nz, nc = r_ref.shape
    filters = w_ref.shape[4]
    rows = (ny + 1) * nz
    plane = r_ref[at_x]
    mine = 1 - at_x
    shifted_copies(plane, shift_ref, 0)
    edge = edge_windows(plane, flat_ref, col_ref, 0, at_y, at_z)
    for p in range(planes):
        lhs = jnp.concatenate([windows(own_ref, source, 1 - at_y, ny) for source in range(planes)], axis=1)
        rhs = w_ref[1 - p : 3 - p].reshape(2 * 9 * nc, filters)
        h_ref[p * rows : (p + 1) * rows] = jnp.dot(lhs, rhs, preferred_element_type=F32)
        lhs = jnp.concatenate([edge_ref[source] for source in range(planes)], axis=1)
        rhs = jnp.concatenate([edge_weights(w_ref, 1 - p, at_z), edge_weights(w_ref, 2 - p, at_z)], axis=0)
        t_ref[p] = jnp.dot(lhs, rhs, preferred_element_type=F32)
    lhs = windows(shift_ref, 0, 1 - at_y, ny)
    rhs = w_ref[2 * mine].reshape(9 * nc, filters)
    begin = pl.multiple_of(mine * rows, 8)
    h_ref[pl.ds(begin, rows)] += jnp.dot(lhs, rhs, preferred_element_type=F32)
    t_ref[mine] += jnp.dot(edge, edge_weights(w_ref, 2 * mine, at_z), preferred_element_type=F32)

    def row(p, e):
        return h_ref[pl.ds(pl.multiple_of((p * (ny + 1) + e) * nz, 8), nz)]

    low = -jnp.inf
    y_edge = lax.broadcasted_iota(jnp.int32, (ny, filters), 0) == (ny - 1) * (1 - at_y)
    is_edge = lax.broadcasted_iota(jnp.int32, (nz, filters), 0) == (nz - 1) * (1 - at_z)
    for k in range(ny // 2):
        first = jnp.maximum(row(0, at_y + 2 * k), row(1, at_y + 2 * k))
        second = jnp.maximum(row(0, at_y + 2 * k + 1), row(1, at_y + 2 * k + 1))
        if k == 0:
            first = jnp.where(at_y == 1, low, first)
        if k == ny // 2 - 1:
            second = jnp.where(at_y == 0, low, second)
        both = jnp.where(is_edge, low, jnp.maximum(first, second))
        for half in range(filters // 128):
            pair_ref[half, k * nz : (k + 1) * nz] = both[:, half * 128 : (half + 1) * 128]
    pooled = [
        jnp.maximum(
            pair_ref[half, pl.ds(0, ny * nz // 4, 2), :],
            pair_ref[half, pl.ds(1, ny * nz // 4, 2), :],
        )
        for half in range(filters // 128)
    ]
    cells = ny * nz // 4
    put(out_ref, 0, leaky(jnp.concatenate(pooled, axis=1)))
    for p in range(planes):
        put(out_ref, cells + p * nz, row(p, (ny - 1) * (1 - at_y) + at_y))
        put(out_ref, cells + planes * nz + p * nz, row(p, ny * (1 - at_y)))
        base = cells + 2 * planes * nz
        here = p * (ny + 1) * nz
        column = []
        for half in range(filters // 128):
            part = slice(half * 128, (half + 1) * 128)
            flat = pair_ref.at[half]
            for e in range(ny + 1):
                flat[e * nz : (e + 1) * nz] = h_ref[here + e * nz : here + (e + 1) * nz, part]
            picks = [flat[pl.ds(e * nz + z, ny, nz), :] for e in (0, 1) for z in (0, nz - 1)]
            column.append(
                jnp.where(
                    at_y == 0,
                    jnp.where(at_z == 0, picks[1], picks[0]),
                    jnp.where(at_z == 0, picks[3], picks[2]),
                )
            )
        corner = jnp.where(at_y == 0, t_ref[p, ny : ny + 1], t_ref[p, 0:1])
        column = jnp.where(y_edge, corner, jnp.concatenate(column, axis=1))
        put(out_ref, base + p * ny, column)
        base += planes * ny
        put(out_ref, base + p * ny, jnp.where(at_y == 0, t_ref[p, 0:ny], t_ref[p, 1 : ny + 1]))


def finish_kernel(q0, q1, q2, q3, w_ref, own_ref, other_ref, pack_ref, full_ref, pair_ref, shift_ref, *, ny, nz, planes):
    at_x, at_y, at_z = (lax.axis_index(axis) for axis in GROUP)
    filters = w_ref.shape[3]
    outs = w_ref.shape[4]
    here = 2 * at_y + at_z
    pack_ref[here] = q0[...]
    pack_ref[2 * (1 - at_y) + at_z] = q1[...]
    pack_ref[2 * at_y + 1 - at_z] = q2[...]
    pack_ref[2 * (1 - at_y) + 1 - at_z] = q3[...]
    py, pz = ny // 2, nz // 2
    cells = py * pz
    row_at = cells
    over_y = row_at + planes * nz
    col_at = over_y + planes * nz
    over_z = col_at + planes * ny

    def take(q, first, count):
        return pack_ref[q, first : first + count].astype(F32)

    def halve(v, slot):
        parts = []
        for half in range(filters // 128):
            pair_ref[slot, half] = v[:, half * 128 : (half + 1) * 128]
            count = v.shape[0] // 2
            parts.append(
                jnp.maximum(pair_ref[slot, half, pl.ds(0, count, 2), :], pair_ref[slot, half, pl.ds(1, count, 2), :])
            )
        return jnp.concatenate(parts, axis=1)

    for qy in range(2):
        for qz in range(2):
            q, by_y, by_z, by_both = 2 * qy + qz, 2 * (1 - qy) + qz, 2 * qy + 1 - qz, 2 * (1 - qy) + 1 - qz
            y_edge, z_edge = (ny - 1) * (1 - qy), (nz - 1) * (1 - qz)
            edge_row, edge_col = None, None
            at = lax.broadcasted_iota(jnp.int32, (nz, filters), 0)
            for p in range(planes):
                across = take(by_z, over_z + p * ny, ny)
                corner = take(by_both, col_at + p * ny, ny)[ny - 1 - y_edge : ny - y_edge]
                extra = across[y_edge : y_edge + 1] + corner
                line = take(q, row_at + p * nz, nz) + take(by_y, over_y + p * nz, nz)
                line = jnp.where(at == z_edge, line + extra, line)
                edge_row = line if edge_row is None else jnp.maximum(edge_row, line)
                line = take(q, col_at + p * ny, ny) + across
                edge_col = line if edge_col is None else jnp.maximum(edge_col, line)
            edge_col = jnp.where(at == y_edge, -jnp.inf, edge_col)
            edge_row = leaky(halve(edge_row, 0))
            edge_col = leaky(halve(edge_col, 1))
            pooled = take(q, 0, cells).reshape(py, pz, filters)
            inner = lax.broadcasted_iota(jnp.int32, (py, pz, filters), 1) == (pz - 1) * (1 - qz)
            pooled = jnp.where(inner, jnp.maximum(pooled, edge_col[:, None, :]), pooled)
            inner = lax.broadcasted_iota(jnp.int32, (py, pz, filters), 0) == (py - 1) * (1 - qy)
            pooled = jnp.where(inner, jnp.maximum(pooled, edge_row[None]), pooled)
            full_ref[qy * py : (qy + 1) * py, qz * pz : (qz + 1) * pz] = pooled
    shifted_copies(full_ref[...].astype(BF), shift_ref, 0)
    parts = []
    for dy in range(3):
        for dz in range(3):
            parts.append(shift_ref[dz, 0, 1 + dy : 1 + dy + ny].reshape(ny * nz, filters))
    lhs = jnp.concatenate(parts, axis=1)
    rhs = jnp.concatenate(
        [w_ref[1].reshape(9 * filters, outs), w_ref[2 * at_x].reshape(9 * filters, outs)], axis=1
    )
    sums = jnp.dot(lhs, rhs, preferred_element_type=F32)
    own_ref[...] = sums[:, :outs]
    other_ref[...] = sums[:, outs:]


def load_kernel(from_ref, after_ref, to_ref, sem):
    load = pltpu.make_async_copy(from_ref, to_ref, sem)
    load.start()
    load.wait()


def add_kernel(own_ref, other_ref, out_ref):
    out_ref[...] = (own_ref[...] + other_ref[...]).astype(out_ref.dtype)


def pair_body(volume, conv4_weight, conv5_weight):
    planes, ny, nz, nc = volume.shape
    f4, f5 = conv4_weight.shape[4], conv5_weight.shape[4]

    def swap(x, flips):
        return lax.ppermute(x, GROUP, [(i, i ^ flips) for i in range(8)])

    cost = functools.partial(pl.CostEstimate, transcendentals=0)
    rows = (ny + 1) * nz
    theirs = swap(volume, 4)
    moved, edges, kernel4 = pl.pallas_call(
        prepare_kernel,
        out_shape=(
            jax.ShapeDtypeStruct((3, planes, ny + 4, nz, nc), BF),
            jax.ShapeDtypeStruct((planes, ny + 8, 3 * nc), BF),
            jax.ShapeDtypeStruct(conv4_weight.shape, BF),
        ),
        in_specs=[HBM, HBM],
        out_specs=(VMEM, VMEM, VMEM),
        scratch_shapes=[
            pltpu.VMEM(volume.shape, BF),
            pltpu.VMEM((planes, ny * nz, nc), F32),
            pltpu.VMEM((planes, ny + 24, nc), F32),
            pltpu.SemaphoreType.DMA,
            pltpu.SemaphoreType.DMA,
        ],
        cost_estimate=cost(flops=20 * planes * ny * nz * nc, bytes_accessed=12 * planes * ny * nz * nc),
        compiler_params=PARAMS,
        name="prepare",
    )(*(pltpu.with_memory_space_constraint(x, pltpu.HBM) for x in (volume, conv4_weight)))
    cells = ny * nz // 4
    packed = cells + planes * (2 * nz + 2 * ny)
    pack = pl.pallas_call(
        pack_kernel,
        out_shape=jax.ShapeDtypeStruct((packed, f4), BF),
        in_specs=[VMEM] * 4,
        out_specs=VMEM,
        scratch_shapes=[
            pltpu.VMEM((planes * rows, f4), F32),
            pltpu.VMEM((planes, ny + 8, f4), F32),
            pltpu.VMEM((3, 1, ny + 4, nz, nc), BF),
            pltpu.VMEM((1, ny * nz, nc), F32),
            pltpu.VMEM((1, ny + 24, nc), F32),
            pltpu.VMEM((f4 // 128, rows, 128), F32),
        ],
        cost_estimate=cost(flops=5 * 2 * rows * 9 * nc * f4, bytes_accessed=54 * nc * f4),
        compiler_params=PARAMS,
        name="conv4_pool_pack",
    )(theirs, kernel4, moved, edges)
    kernel5 = pl.pallas_call(
        load_kernel,
        out_shape=jax.ShapeDtypeStruct(conv5_weight.shape, BF),
        in_specs=[HBM, VMEM],
        out_specs=VMEM,
        scratch_shapes=[pltpu.SemaphoreType.DMA],
        cost_estimate=cost(flops=0, bytes_accessed=108 * f4 * f5),
        compiler_params=PARAMS,
        name="load_conv5_weight",
    )(pltpu.with_memory_space_constraint(conv5_weight, pltpu.HBM), pack)
    by_y = swap(pack, 2)
    by_z = swap(pack, 1)
    by_both = swap(pack, 3)
    gy, gz = 2 * ny // 2, 2 * nz // 2
    own, other = pl.pallas_call(
        functools.partial(finish_kernel, ny=ny, nz=nz, planes=planes),
        out_shape=(jax.ShapeDtypeStruct((gy * gz, f5), F32), jax.ShapeDtypeStruct((gy * gz, f5), F32)),
        in_specs=[VMEM] * 5,
        out_specs=(VMEM, VMEM),
        scratch_shapes=[
            pltpu.VMEM((4, packed, f4), BF),
            pltpu.VMEM((gy, gz, f4), F32),
            pltpu.VMEM((2, f4 // 128, max(ny, nz), 128), F32),
            pltpu.VMEM((3, 1, gy + 4, gz, f4), BF),
        ],
        cost_estimate=cost(flops=4 * gy * gz * 9 * f4 * f5, bytes_accessed=36 * f4 * f5),
        compiler_params=PARAMS,
        name="finish_and_conv5",
    )(pack, by_y, by_z, by_both, kernel5)
    features = pl.pallas_call(
        add_kernel,
        out_shape=jax.ShapeDtypeStruct((gy * gz, f5), BF),
        in_specs=[VMEM] * 2,
        out_specs=VMEM,
        compiler_params=PARAMS,
        name="add_planes",
    )(own, swap(other, 4))
    return features.reshape(1, gy, gz, f5)


def body(volume, conv4_weight, conv5_weight):
    if all(lax.axis_size(axis) == 2 for axis in GROUP) and volume.shape[0] == 2:
        return pair_body(volume, conv4_weight, conv5_weight)
    return general_body(volume, conv4_weight, conv5_weight)


def solution(mesh):
    return jax.shard_map(
        body,
        mesh=mesh,
        in_specs=(
            P(("sample", "gx"), "gy", "gz", None),
            P(),
            P(None, None, None, None, ("gy", "gz")),
        ),
        out_specs=P(("sample", "gx"), None, None, ("gy", "gz")),
        check_vma=False,
    )
```

```python
import functools

import jax
import jax.numpy as jnp
from jax import lax
from jax.experimental import pallas as pl
from jax.experimental.pallas import tpu as pltpu
from jax.sharding import PartitionSpec as P

BF = jnp.bfloat16
F32 = jnp.float32
VMEM = pl.BlockSpec(memory_space=pltpu.VMEM)
HBM = pl.BlockSpec(memory_space=pltpu.HBM)
GROUP = ("gx", "gy", "gz")
PARAMS = pltpu.CompilerParams(vmem_limit_bytes=8 * 2**20)


def extended(cells, sides, width):
    for axis, dim in sides:
        count = lax.axis_size(axis)
        ends = count - 1
        head = lax.slice_in_dim(cells, 0, width, axis=dim)
        tail = lax.slice_in_dim(cells, cells.shape[dim] - width, cells.shape[dim], axis=dim)
        cells = jnp.concatenate(
            [
                lax.ppermute(tail, axis, [(i, (i + 1) % count) for i in range(ends)]),
                cells,
                lax.ppermute(head, axis, [((i + 1) % count, i) for i in range(ends)]),
            ],
            axis=dim,
        )
    return cells


def conv_local(padded, kernel):
    extent_x = padded.shape[0] - 2
    extent_y = padded.shape[1] - 2
    extent_z = padded.shape[2] - 2
    inputs = padded.shape[3]
    summed = None
    for along_x in range(3):
        for along_y in range(3):
            for along_z in range(3):
                window = padded[
                    along_x : along_x + extent_x,
                    along_y : along_y + extent_y,
                    along_z : along_z + extent_z,
                ]
                window = window.reshape(extent_x * extent_y * extent_z, inputs)
                contrib = jnp.dot(
                    window, kernel[along_x, along_y, along_z], preferred_element_type=jnp.float32
                )
                summed = contrib if summed is None else summed + contrib
    return summed.reshape(extent_x, extent_y, extent_z, kernel.shape[4])


def pool_leaky(hidden):
    leaked = jnp.where(hidden > 0, hidden, 0.3 * hidden)
    sizes = leaked.shape
    blocks = leaked.reshape(sizes[0] // 2, 2, sizes[1] // 2, 2, sizes[2] // 2, 2, sizes[3])
    return jnp.max(blocks, axis=(1, 3, 5)).astype(jnp.bfloat16)


def general_body(volume, conv4_weight, conv5_weight):
    padded = extended(volume, (("gx", 0), ("gy", 1), ("gz", 2)), 1)
    pooled = pool_leaky(conv_local(padded, conv4_weight))
    strips = lax.all_gather(pooled, "gz", axis=2, tiled=True)
    slab = lax.all_gather(strips, "gy", axis=1, tiled=True)
    bordered = extended(slab, (("gx", 0),), 1)
    bordered = jnp.pad(bordered, ((0, 0), (1, 1), (1, 1), (0, 0)))
    return conv_local(bordered, conv5_weight).astype(jnp.bfloat16)


def leaky(v):
    return jnp.where(v > 0, v, 0.3 * v)


def shifted_copies(plane, out_ref, index):
    ny, nz, nc = plane.shape
    flat = plane.reshape(ny * nz, nc).astype(F32)
    at = lax.broadcasted_iota(jnp.int32, flat.shape, 0) % nz
    after = jnp.where(at == 0, 0.0, pltpu.roll(flat, 1, 0))
    before = jnp.where(at == nz - 1, 0.0, pltpu.roll(flat, ny * nz - 1, 0))
    none = jnp.zeros((2, nz, nc), BF)
    for dz, moved in enumerate((after, flat, before)):
        out_ref[dz, index, 0:2] = none
        out_ref[dz, index, 2 + ny : 4 + ny] = none
        out_ref[dz, index, 2 : 2 + ny] = moved.astype(BF).reshape(ny, nz, nc)


def windows(shift_ref, index, first, ny):
    nz, nc = shift_ref.shape[3:]
    parts = []
    for dy in range(3):
        for dz in range(3):
            part = shift_ref[dz, index, pl.ds(first + dy, ny + 1)]
            parts.append(part.reshape((ny + 1) * nz, nc))
    return jnp.concatenate(parts, axis=1)


def edge_windows(plane, flat_ref, col_ref, index, at_y, at_z):
    ny, nz, nc = plane.shape
    flat_ref[index] = plane.reshape(ny * nz, nc).astype(F32)
    low = flat_ref[index, pl.ds(0, ny, nz), :]
    high = flat_ref[index, pl.ds(nz - 1, ny, nz), :]
    col_ref[index] = jnp.zeros(col_ref.shape[1:], F32)
    col_ref[index, 8 : 8 + ny] = jnp.where(at_z == 0, high, low)
    parts = []
    for dy in range(3):
        near = col_ref[index, 7 + dy : 15 + dy + ny]
        far = col_ref[index, 6 + dy : 14 + dy + ny]
        parts.append(jnp.where(at_y == 0, near, far).astype(BF))
    return jnp.concatenate(parts, axis=1)


def edge_weights(w_ref, dx, at_z):
    taps = w_ref.shape[1]
    return jnp.concatenate([w_ref[dx, dy, 2 * at_z] for dy in range(taps)], axis=0)


def prepare_kernel(v_hbm, w_hbm, shift_ref, edge_ref, w_ref, v_ref, flat_ref, col_ref, v_sem, w_sem):
    load_v = pltpu.make_async_copy(v_hbm, v_ref, v_sem)
    load_w = pltpu.make_async_copy(w_hbm, w_ref, w_sem)
    load_v.start()
    load_w.start()
    at_y, at_z = lax.axis_index("gy"), lax.axis_index("gz")
    load_v.wait()
    for p in range(v_ref.shape[0]):
        shifted_copies(v_ref[p], shift_ref, p)
        edge_ref[p] = edge_windows(v_ref[p], flat_ref, col_ref, p, at_y, at_z)
    load_w.wait()


def put(out_ref, first, rows):
    out_ref[first : first + rows.shape[0]] = rows.astype(out_ref.dtype)


def pack_kernel(r_ref, w_ref, own_ref, edge_ref, out_ref, h_ref, t_ref, shift_ref, flat_ref, col_ref, pair_ref):
    at_x, at_y, at_z = (lax.axis_index(axis) for axis in GROUP)
    planes, ny, nz, nc = r_ref.shape
    filters = w_ref.shape[4]
    rows = (ny + 1) * nz
    plane = r_ref[at_x]
    mine = 1 - at_x
    shifted_copies(plane, shift_ref, 0)
    edge = edge_windows(plane, flat_ref, col_ref, 0, at_y, at_z)
    for p in range(planes):
        lhs = jnp.concatenate([windows(own_ref, source, 1 - at_y, ny) for source in range(planes)], axis=1)
        rhs = w_ref[1 - p : 3 - p].reshape(2 * 9 * nc, filters)
        h_ref[p * rows : (p + 1) * rows] = jnp.dot(lhs, rhs, preferred_element_type=F32)
        lhs = jnp.concatenate([edge_ref[source] for source in range(planes)], axis=1)
        rhs = jnp.concatenate([edge_weights(w_ref, 1 - p, at_z), edge_weights(w_ref, 2 - p, at_z)], axis=0)
        t_ref[p] = jnp.dot(lhs, rhs, preferred_element_type=F32)
    lhs = windows(shift_ref, 0, 1 - at_y, ny)
    rhs = w_ref[2 * mine].reshape(9 * nc, filters)
    begin = pl.multiple_of(mine * rows, 8)
    h_ref[pl.ds(begin, rows)] += jnp.dot(lhs, rhs, preferred_element_type=F32)
    t_ref[mine] += jnp.dot(edge, edge_weights(w_ref, 2 * mine, at_z), preferred_element_type=F32)

    def row(p, e):
        return h_ref[pl.ds(pl.multiple_of((p * (ny + 1) + e) * nz, 8), nz)]

    low = -jnp.inf
    y_edge = lax.broadcasted_iota(jnp.int32, (ny, filters), 0) == (ny - 1) * (1 - at_y)
    is_edge = lax.broadcasted_iota(jnp.int32, (nz, filters), 0) == (nz - 1) * (1 - at_z)
    for k in range(ny // 2):
        first = jnp.maximum(row(0, at_y + 2 * k), row(1, at_y + 2 * k))
        second = jnp.maximum(row(0, at_y + 2 * k + 1), row(1, at_y + 2 * k + 1))
        if k == 0:
            first = jnp.where(at_y == 1, low, first)
        if k == ny // 2 - 1:
            second = jnp.where(at_y == 0, low, second)
        both = jnp.where(is_edge, low, jnp.maximum(first, second))
        for half in range(filters // 128):
            pair_ref[half, k * nz : (k + 1) * nz] = both[:, half * 128 : (half + 1) * 128]
    pooled = [
        jnp.maximum(
            pair_ref[half, pl.ds(0, ny * nz // 4, 2), :],
            pair_ref[half, pl.ds(1, ny * nz // 4, 2), :],
        )
        for half in range(filters // 128)
    ]
    cells = ny * nz // 4
    put(out_ref, 0, leaky(jnp.concatenate(pooled, axis=1)))
    for p in range(planes):
        put(out_ref, cells + p * nz, row(p, (ny - 1) * (1 - at_y) + at_y))
        put(out_ref, cells + planes * nz + p * nz, row(p, ny * (1 - at_y)))
        base = cells + 2 * planes * nz
        here = p * (ny + 1) * nz
        column = []
        for half in range(filters // 128):
            part = slice(half * 128, (half + 1) * 128)
            flat = pair_ref.at[half]
            for e in range(ny + 1):
                flat[e * nz : (e + 1) * nz] = h_ref[here + e * nz : here + (e + 1) * nz, part]
            picks = [flat[pl.ds(e * nz + z, ny, nz), :] for e in (0, 1) for z in (0, nz - 1)]
            column.append(
                jnp.where(
                    at_y == 0,
                    jnp.where(at_z == 0, picks[1], picks[0]),
                    jnp.where(at_z == 0, picks[3], picks[2]),
                )
            )
        corner = jnp.where(at_y == 0, t_ref[p, ny : ny + 1], t_ref[p, 0:1])
        column = jnp.where(y_edge, corner, jnp.concatenate(column, axis=1))
        put(out_ref, base + p * ny, column)
        base += planes * ny
        put(out_ref, base + p * ny, jnp.where(at_y == 0, t_ref[p, 0:ny], t_ref[p, 1 : ny + 1]))


def finish_kernel(q0, q1, q2, q3, w_ref, own_ref, other_ref, pack_ref, full_ref, pair_ref, shift_ref, *, ny, nz, planes):
    at_x, at_y, at_z = (lax.axis_index(axis) for axis in GROUP)
    filters = w_ref.shape[3]
    outs = w_ref.shape[4]
    here = 2 * at_y + at_z
    pack_ref[here] = q0[...]
    pack_ref[2 * (1 - at_y) + at_z] = q1[...]
    pack_ref[2 * at_y + 1 - at_z] = q2[...]
    pack_ref[2 * (1 - at_y) + 1 - at_z] = q3[...]
    py, pz = ny // 2, nz // 2
    cells = py * pz
    row_at = cells
    over_y = row_at + planes * nz
    col_at = over_y + planes * nz
    over_z = col_at + planes * ny

    def take(q, first, count):
        return pack_ref[q, first : first + count].astype(F32)

    def halve(v, slot):
        parts = []
        for half in range(filters // 128):
            pair_ref[slot, half] = v[:, half * 128 : (half + 1) * 128]
            count = v.shape[0] // 2
            parts.append(
                jnp.maximum(pair_ref[slot, half, pl.ds(0, count, 2), :], pair_ref[slot, half, pl.ds(1, count, 2), :])
            )
        return jnp.concatenate(parts, axis=1)

    for qy in range(2):
        for qz in range(2):
            q, by_y, by_z, by_both = 2 * qy + qz, 2 * (1 - qy) + qz, 2 * qy + 1 - qz, 2 * (1 - qy) + 1 - qz
            y_edge, z_edge = (ny - 1) * (1 - qy), (nz - 1) * (1 - qz)
            edge_row, edge_col = None, None
            at = lax.broadcasted_iota(jnp.int32, (nz, filters), 0)
            for p in range(planes):
                across = take(by_z, over_z + p * ny, ny)
                corner = take(by_both, col_at + p * ny, ny)[ny - 1 - y_edge : ny - y_edge]
                extra = across[y_edge : y_edge + 1] + corner
                line = take(q, row_at + p * nz, nz) + take(by_y, over_y + p * nz, nz)
                line = jnp.where(at == z_edge, line + extra, line)
                edge_row = line if edge_row is None else jnp.maximum(edge_row, line)
                line = take(q, col_at + p * ny, ny) + across
                edge_col = line if edge_col is None else jnp.maximum(edge_col, line)
            edge_col = jnp.where(at == y_edge, -jnp.inf, edge_col)
            edge_row = leaky(halve(edge_row, 0))
            edge_col = leaky(halve(edge_col, 1))
            pooled = take(q, 0, cells).reshape(py, pz, filters)
            inner = lax.broadcasted_iota(jnp.int32, (py, pz, filters), 1) == (pz - 1) * (1 - qz)
            pooled = jnp.where(inner, jnp.maximum(pooled, edge_col[:, None, :]), pooled)
            inner = lax.broadcasted_iota(jnp.int32, (py, pz, filters), 0) == (py - 1) * (1 - qy)
            pooled = jnp.where(inner, jnp.maximum(pooled, edge_row[None]), pooled)
            full_ref[qy * py : (qy + 1) * py, qz * pz : (qz + 1) * pz] = pooled
    shifted_copies(full_ref[...].astype(BF), shift_ref, 0)
    parts = []
    for dy in range(3):
        for dz in range(3):
            parts.append(shift_ref[dz, 0, 1 + dy : 1 + dy + ny].reshape(ny * nz, filters))
    lhs = jnp.concatenate(parts, axis=1)
    rhs = jnp.concatenate(
        [w_ref[1].reshape(9 * filters, outs), w_ref[2 * at_x].reshape(9 * filters, outs)], axis=1
    )
    sums = jnp.dot(lhs, rhs, preferred_element_type=F32)
    own_ref[...] = sums[:, :outs]
    other_ref[...] = sums[:, outs:].astype(other_ref.dtype)


def add_kernel(own_ref, other_ref, out_ref):
    out_ref[...] = (own_ref[...] + other_ref[...]).astype(out_ref.dtype)


def pair_body(volume, conv4_weight, conv5_weight):
    planes, ny, nz, nc = volume.shape
    f4, f5 = conv4_weight.shape[4], conv5_weight.shape[4]

    def swap(x, flips):
        return lax.ppermute(x, GROUP, [(i, i ^ flips) for i in range(8)])

    cost = functools.partial(pl.CostEstimate, transcendentals=0)
    rows = (ny + 1) * nz
    theirs = swap(volume, 4)
    moved, edges, kernel4 = pl.pallas_call(
        prepare_kernel,
        out_shape=(
            jax.ShapeDtypeStruct((3, planes, ny + 4, nz, nc), BF),
            jax.ShapeDtypeStruct((planes, ny + 8, 3 * nc), BF),
            jax.ShapeDtypeStruct(conv4_weight.shape, BF),
        ),
        in_specs=[HBM, HBM],
        out_specs=(VMEM, VMEM, VMEM),
        scratch_shapes=[
            pltpu.VMEM(volume.shape, BF),
            pltpu.VMEM((planes, ny * nz, nc), F32),
            pltpu.VMEM((planes, ny + 24, nc), F32),
            pltpu.SemaphoreType.DMA,
            pltpu.SemaphoreType.DMA,
        ],
        cost_estimate=cost(flops=20 * planes * ny * nz * nc, bytes_accessed=12 * planes * ny * nz * nc),
        compiler_params=PARAMS,
        name="prepare",
    )(*(pltpu.with_memory_space_constraint(x, pltpu.HBM) for x in (volume, conv4_weight)))
    cells = ny * nz // 4
    packed = cells + planes * (2 * nz + 2 * ny)
    pack = pl.pallas_call(
        pack_kernel,
        out_shape=jax.ShapeDtypeStruct((packed, f4), BF),
        in_specs=[VMEM] * 4,
        out_specs=VMEM,
        scratch_shapes=[
            pltpu.VMEM((planes * rows, f4), F32),
            pltpu.VMEM((planes, ny + 8, f4), F32),
            pltpu.VMEM((3, 1, ny + 4, nz, nc), BF),
            pltpu.VMEM((1, ny * nz, nc), F32),
            pltpu.VMEM((1, ny + 24, nc), F32),
            pltpu.VMEM((f4 // 128, rows, 128), F32),
        ],
        cost_estimate=cost(flops=5 * 2 * rows * 9 * nc * f4, bytes_accessed=54 * nc * f4),
        compiler_params=PARAMS,
        name="conv4_pool_pack",
    )(theirs, kernel4, moved, edges)
    by_y = swap(pack, 2)
    by_z = swap(pack, 1)
    by_both = swap(pack, 3)
    gy, gz = 2 * ny // 2, 2 * nz // 2
    own, other = pl.pallas_call(
        functools.partial(finish_kernel, ny=ny, nz=nz, planes=planes),
        out_shape=(jax.ShapeDtypeStruct((gy * gz, f5), F32), jax.ShapeDtypeStruct((gy * gz, f5), BF)),
        in_specs=[VMEM] * 5,
        out_specs=(VMEM, VMEM),
        scratch_shapes=[
            pltpu.VMEM((4, packed, f4), BF),
            pltpu.VMEM((gy, gz, f4), F32),
            pltpu.VMEM((2, f4 // 128, max(ny, nz), 128), F32),
            pltpu.VMEM((3, 1, gy + 4, gz, f4), BF),
        ],
        cost_estimate=cost(flops=4 * gy * gz * 9 * f4 * f5, bytes_accessed=36 * f4 * f5),
        compiler_params=PARAMS,
        name="finish_and_conv5",
    )(pack, by_y, by_z, by_both, conv5_weight)
    features = pl.pallas_call(
        add_kernel,
        out_shape=jax.ShapeDtypeStruct((gy * gz, f5), BF),
        in_specs=[VMEM] * 2,
        out_specs=VMEM,
        compiler_params=PARAMS,
        name="add_planes",
    )(own, swap(other, 4))
    return features.reshape(1, gy, gz, f5)


def body(volume, conv4_weight, conv5_weight):
    if all(lax.axis_size(axis) == 2 for axis in GROUP) and volume.shape[0] == 2:
        return pair_body(volume, conv4_weight, conv5_weight)
    return general_body(volume, conv4_weight, conv5_weight)


def solution(mesh):
    return jax.shard_map(
        body,
        mesh=mesh,
        in_specs=(
            P(("sample", "gx"), "gy", "gz", None),
            P(),
            P(None, None, None, None, ("gy", "gz")),
        ),
        out_specs=P(("sample", "gx"), None, None, ("gy", "gz")),
        check_vma=False,
    )
```

```python
import functools

import jax
import jax.numpy as jnp
from jax import lax
from jax.experimental import pallas as pl
from jax.experimental.pallas import tpu as pltpu
from jax.sharding import PartitionSpec as P

BF = jnp.bfloat16
F32 = jnp.float32
VMEM = pl.BlockSpec(memory_space=pltpu.VMEM)
HBM = pl.BlockSpec(memory_space=pltpu.HBM)
GROUP = ("gx", "gy", "gz")
PARAMS = pltpu.CompilerParams(vmem_limit_bytes=8 * 2**20)


def extended(cells, sides, width):
    for axis, dim in sides:
        count = lax.axis_size(axis)
        ends = count - 1
        head = lax.slice_in_dim(cells, 0, width, axis=dim)
        tail = lax.slice_in_dim(cells, cells.shape[dim] - width, cells.shape[dim], axis=dim)
        cells = jnp.concatenate(
            [
                lax.ppermute(tail, axis, [(i, (i + 1) % count) for i in range(ends)]),
                cells,
                lax.ppermute(head, axis, [((i + 1) % count, i) for i in range(ends)]),
            ],
            axis=dim,
        )
    return cells


def conv_local(padded, kernel):
    extent_x = padded.shape[0] - 2
    extent_y = padded.shape[1] - 2
    extent_z = padded.shape[2] - 2
    inputs = padded.shape[3]
    summed = None
    for along_x in range(3):
        for along_y in range(3):
            for along_z in range(3):
                window = padded[
                    along_x : along_x + extent_x,
                    along_y : along_y + extent_y,
                    along_z : along_z + extent_z,
                ]
                window = window.reshape(extent_x * extent_y * extent_z, inputs)
                contrib = jnp.dot(
                    window, kernel[along_x, along_y, along_z], preferred_element_type=jnp.float32
                )
                summed = contrib if summed is None else summed + contrib
    return summed.reshape(extent_x, extent_y, extent_z, kernel.shape[4])


def pool_leaky(hidden):
    leaked = jnp.where(hidden > 0, hidden, 0.3 * hidden)
    sizes = leaked.shape
    blocks = leaked.reshape(sizes[0] // 2, 2, sizes[1] // 2, 2, sizes[2] // 2, 2, sizes[3])
    return jnp.max(blocks, axis=(1, 3, 5)).astype(jnp.bfloat16)


def general_body(volume, conv4_weight, conv5_weight):
    padded = extended(volume, (("gx", 0), ("gy", 1), ("gz", 2)), 1)
    pooled = pool_leaky(conv_local(padded, conv4_weight))
    strips = lax.all_gather(pooled, "gz", axis=2, tiled=True)
    slab = lax.all_gather(strips, "gy", axis=1, tiled=True)
    bordered = extended(slab, (("gx", 0),), 1)
    bordered = jnp.pad(bordered, ((0, 0), (1, 1), (1, 1), (0, 0)))
    return conv_local(bordered, conv5_weight).astype(jnp.bfloat16)


def leaky(v):
    return jnp.where(v > 0, v, 0.3 * v)


def shifted_copies(plane, out_ref, index, border):
    ny, nz, nc = plane.shape
    flat = plane.reshape(ny * nz, nc).astype(F32)
    at = lax.broadcasted_iota(jnp.int32, flat.shape, 0) % nz
    after = jnp.where(at == 0, 0.0, pltpu.roll(flat, 1, 0))
    before = jnp.where(at == nz - 1, 0.0, pltpu.roll(flat, ny * nz - 1, 0))
    for dz, moved in enumerate((after, flat, before)):
        if border:
            out_ref[dz, index, 0:border] = jnp.zeros((border, nz, nc), BF)
            out_ref[dz, index, border + ny : 2 * border + ny] = jnp.zeros((border, nz, nc), BF)
        out_ref[dz, index, border : border + ny] = moved.astype(BF).reshape(ny, nz, nc)


def windows(shift_ref, index, first, count):
    nz, nc = shift_ref.shape[3:]
    parts = []
    for dy in range(3):
        for dz in range(3):
            parts.append(shift_ref[dz, index, first + dy : first + dy + count].reshape(count * nz, nc))
    return jnp.concatenate(parts, axis=1)


def edge_columns(plane, flat_ref, at_z):
    ny, nz, nc = plane.shape
    flat_ref[...] = plane.reshape(ny * nz, nc).astype(F32)
    low = [flat_ref[pl.ds(z, ny, nz), :] for z in (0, 1)]
    high = [flat_ref[pl.ds(z, ny, nz), :] for z in (nz - 2, nz - 1)]
    return jnp.where(at_z == 0, jnp.concatenate(high, axis=1), jnp.concatenate(low, axis=1)).astype(BF)


def prepare_kernel(v_hbm, w_hbm, shift_ref, column_ref, w_ref, v_ref, flat_ref, v_sem, w_sem):
    load_v = pltpu.make_async_copy(v_hbm, v_ref, v_sem)
    load_w = pltpu.make_async_copy(w_hbm, w_ref, w_sem)
    load_v.start()
    load_w.start()
    at_z = lax.axis_index("gz")
    load_v.wait()
    for p in range(v_ref.shape[0]):
        shifted_copies(v_ref[p], shift_ref, p, 1)
        column_ref[p] = edge_columns(v_ref[p], flat_ref, at_z)
    load_w.wait()


def pack_kernel(r_ref, w_ref, own_ref, column_ref, out_ref, h_ref, shift_ref, flat_ref, pair_ref):
    at_x, at_y, at_z = (lax.axis_index(axis) for axis in GROUP)
    planes, ny, nz, nc = r_ref.shape
    filters = w_ref.shape[4]
    rows = ny * nz
    plane = r_ref[at_x]
    mine = 1 - at_x
    shifted_copies(plane, shift_ref, 0, 1)
    cells = ny * nz // 4
    columns = cells + (planes + 1) * nz
    first_row = (ny - 2) * (1 - at_y) + 1

    def put_edges(slot, source_ref, index, column):
        begin = pl.multiple_of(cells + slot * nz, 16)
        near = [source_ref[1, index, first_row + side] for side in range(2)]
        out_ref[pl.ds(begin, nz)] = jnp.concatenate(near, axis=1)
        begin = pl.multiple_of(columns + slot * ny, 16)
        out_ref[pl.ds(begin, ny)] = column

    put_edges(2 * mine, shift_ref, 0, edge_columns(plane, flat_ref, at_z))
    for p in range(planes):
        put_edges(at_x + p, own_ref, p, column_ref[p])
    step = 8
    for first in range(0, ny, step):
        lhs = jnp.concatenate([windows(own_ref, source, first, step) for source in range(planes)], axis=1)
        halo = windows(shift_ref, 0, first, step)
        sums = jnp.dot(lhs, w_ref[pl.ds(at_x, planes)].reshape(planes * 9 * nc, filters), preferred_element_type=F32)
        sums += jnp.dot(halo, w_ref[2 * mine].reshape(9 * nc, filters), preferred_element_type=F32)
        rest = w_ref[pl.ds(mine, planes)].reshape(planes * 9 * nc, filters)
        h_ref[first * nz : (first + step) * nz] = jnp.maximum(sums, jnp.dot(lhs, rest, preferred_element_type=F32))

    def row(y):
        return h_ref[y * nz : (y + 1) * nz]

    low = -jnp.inf
    is_edge = lax.broadcasted_iota(jnp.int32, (nz, filters), 0) == (nz - 1) * (1 - at_z)
    for k in range(ny // 2):
        first, second = row(2 * k), row(2 * k + 1)
        if k == 0:
            first = jnp.where(at_y == 1, low, first)
        if k == ny // 2 - 1:
            second = jnp.where(at_y == 0, low, second)
        both = jnp.where(is_edge, low, jnp.maximum(first, second))
        for half in range(filters // 128):
            pair_ref[half, k * nz : (k + 1) * nz] = both[:, half * 128 : (half + 1) * 128]
    pooled = [
        jnp.maximum(pair_ref[half, pl.ds(0, cells, 2), :], pair_ref[half, pl.ds(1, cells, 2), :])
        for half in range(filters // 128)
    ]
    out_ref[0:cells] = leaky(jnp.concatenate(pooled, axis=1)).astype(out_ref.dtype)


def finish_kernel(
    q0, q1, q2, q3, w4_ref, w_ref, own_ref, other_ref, pack_ref, cross_ref, h_ref, full_ref, pair_ref, shift_ref, *, ny, nz, planes
):
    at_x, at_y, at_z = (lax.axis_index(axis) for axis in GROUP)
    mine = 1 - at_x
    filters = w_ref.shape[3]
    outs = w_ref.shape[4]
    nc = w4_ref.shape[3]
    here = 2 * at_y + at_z
    pack_ref[here] = q0[...]
    pack_ref[2 * (1 - at_y) + at_z] = q1[...]
    pack_ref[2 * at_y + 1 - at_z] = q2[...]
    pack_ref[2 * (1 - at_y) + 1 - at_z] = q3[...]
    py, pz = ny // 2, nz // 2
    cells = py * pz
    columns = cells + (planes + 1) * nz

    for slot in range(planes + 1):
        lines = []
        for side in range(4):
            lanes = slice(side % 2 * nc, side % 2 * nc + nc)
            begin = cells + slot * nz
            parts = [pack_ref[2 * (side // 2) + qz, begin : begin + nz, lanes] for qz in range(2)]
            lines.append(jnp.concatenate(parts, axis=0)[None])
        shifted_copies(jnp.concatenate(lines, axis=0), cross_ref.at[0], slot, 0)
        lines = []
        for side in range(4):
            lanes = slice(side % 2 * nc, side % 2 * nc + nc)
            begin = columns + slot * ny
            parts = [pack_ref[2 * qy + side // 2, begin : begin + ny, lanes] for qy in range(2)]
            lines.append(jnp.concatenate(parts, axis=0)[None])
        shifted_copies(jnp.concatenate(lines, axis=0), cross_ref.at[1], slot, 0)

    def cross_windows(kind, slot):
        parts = []
        for dy in range(3):
            for dz in range(3):
                along, over = (dz, dy) if kind == 0 else (dy, dz)
                part = cross_ref[kind, along, slot, over : over + 2]
                parts.append(part.reshape(part.shape[0] * part.shape[1], nc))
        return jnp.concatenate(parts, axis=1)

    wins = [jnp.concatenate([cross_windows(kind, slot) for kind in range(2)], axis=0) for slot in range(planes + 1)]
    rhs = w4_ref[...].reshape((planes + 1) * 9 * nc, filters)
    inner = jnp.dot(jnp.concatenate(wins, axis=1), rhs, preferred_element_type=F32)
    wins = [
        jnp.concatenate([cross_windows(kind, at_x + p) for kind in range(2)], axis=0) for p in range(planes)
    ]
    rhs = w4_ref[pl.ds(mine, planes)].reshape(planes * 9 * nc, filters)
    h_ref[...] = jnp.maximum(inner, jnp.dot(jnp.concatenate(wins, axis=1), rhs, preferred_element_type=F32))

    def halve(v, slot):
        parts = []
        for half in range(filters // 128):
            pair_ref[slot, half] = v[:, half * 128 : (half + 1) * 128]
            count = v.shape[0] // 2
            parts.append(
                jnp.maximum(pair_ref[slot, half, pl.ds(0, count, 2), :], pair_ref[slot, half, pl.ds(1, count, 2), :])
            )
        return jnp.concatenate(parts, axis=1)

    for qy in range(2):
        for qz in range(2):
            pooled = pack_ref[2 * qy + qz, 0:cells].astype(F32)
            full_ref[qy * py : (qy + 1) * py, qz * pz : (qz + 1) * pz] = pooled.reshape(py, pz, filters)
    pooled = full_ref[...]
    at_row = lax.broadcasted_iota(jnp.int32, (2 * py, 1, filters), 0)
    at_col = lax.broadcasted_iota(jnp.int32, (1, 2 * pz, filters), 1)
    for side in range(2):
        first = side * 2 * nz
        line = h_ref[first : first + 2 * nz]
        line = leaky(halve(line, side))
        pooled = jnp.maximum(pooled, jnp.where(at_row == py - 1 + side, line[None], -jnp.inf))
        first = 4 * nz + side * 2 * ny
        line = h_ref[first : first + 2 * ny]
        line = leaky(halve(line, 2 + side))
        pooled = jnp.maximum(pooled, jnp.where(at_col == pz - 1 + side, line[:, None, :], -jnp.inf))
    shifted_copies(pooled.astype(BF), shift_ref, 0, 1)
    rhs = jnp.concatenate(
        [w_ref[1].reshape(9 * filters, outs), w_ref[2 * at_x].reshape(9 * filters, outs)], axis=1
    )
    step = 8
    for first in range(0, ny, step):
        sums = jnp.dot(windows(shift_ref, 0, first, step), rhs, preferred_element_type=F32)
        own_ref[first * nz : (first + step) * nz] = sums[:, :outs]
        other_ref[first * nz : (first + step) * nz] = sums[:, outs:].astype(other_ref.dtype)


def add_kernel(own_ref, other_ref, out_ref):
    out_ref[...] = (own_ref[...] + other_ref[...]).astype(out_ref.dtype)


def pair_body(volume, conv4_weight, conv5_weight):
    planes, ny, nz, nc = volume.shape
    f4, f5 = conv4_weight.shape[4], conv5_weight.shape[4]

    def swap(x, flips):
        return lax.ppermute(x, GROUP, [(i, i ^ flips) for i in range(8)])

    cost = functools.partial(pl.CostEstimate, transcendentals=0)
    rows = ny * nz
    theirs = swap(volume, 4)
    moved, columns, kernel4 = pl.pallas_call(
        prepare_kernel,
        out_shape=(
            jax.ShapeDtypeStruct((3, planes, ny + 2, nz, nc), BF),
            jax.ShapeDtypeStruct((planes, ny, 2 * nc), BF),
            jax.ShapeDtypeStruct(conv4_weight.shape, BF),
        ),
        in_specs=[HBM, HBM],
        out_specs=(VMEM, VMEM, VMEM),
        scratch_shapes=[
            pltpu.VMEM(volume.shape, BF),
            pltpu.VMEM((rows, nc), F32),
            pltpu.SemaphoreType.DMA,
            pltpu.SemaphoreType.DMA,
        ],
        cost_estimate=cost(flops=20 * planes * rows * nc, bytes_accessed=54 * nc * f4),
        compiler_params=PARAMS,
        name="prepare",
    )(*(pltpu.with_memory_space_constraint(x, pltpu.HBM) for x in (volume, conv4_weight)))
    packed = rows // 4 + (planes + 1) * (ny + nz)
    pack = pl.pallas_call(
        pack_kernel,
        out_shape=jax.ShapeDtypeStruct((packed, f4), BF),
        in_specs=[VMEM] * 4,
        out_specs=VMEM,
        scratch_shapes=[
            pltpu.VMEM((rows, f4), F32),
            pltpu.VMEM((3, 1, ny + 2, nz, nc), BF),
            pltpu.VMEM((rows, nc), F32),
            pltpu.VMEM((f4 // 128, rows // 2, 128), F32),
        ],
        cost_estimate=cost(flops=5 * 2 * rows * 9 * nc * f4, bytes_accessed=54 * nc * f4),
        compiler_params=PARAMS,
        name="conv4_pool_pack",
    )(theirs, kernel4, moved, columns)
    by_y = swap(pack, 2)
    by_z = swap(pack, 1)
    by_both = swap(pack, 3)
    gy, gz = 2 * ny // 2, 2 * nz // 2
    own, other = pl.pallas_call(
        functools.partial(finish_kernel, ny=ny, nz=nz, planes=planes),
        out_shape=(jax.ShapeDtypeStruct((gy * gz, f5), F32), jax.ShapeDtypeStruct((gy * gz, f5), BF)),
        in_specs=[VMEM] * 6,
        out_specs=(VMEM, VMEM),
        scratch_shapes=[
            pltpu.VMEM((4, packed, f4), BF),
            pltpu.VMEM((2, 3, planes + 1, 4, 2 * nz, nc), BF),
            pltpu.VMEM((4 * ny + 4 * nz, f4), F32),
            pltpu.VMEM((gy, gz, f4), F32),
            pltpu.VMEM((4, f4 // 128, 2 * nz, 128), F32),
            pltpu.VMEM((3, 1, gy + 2, gz, f4), BF),
        ],
        cost_estimate=cost(flops=4 * gy * gz * 9 * f4 * f5, bytes_accessed=36 * f4 * f5),
        compiler_params=PARAMS,
        name="finish_and_conv5",
    )(pack, by_y, by_z, by_both, kernel4, conv5_weight)
    features = pl.pallas_call(
        add_kernel,
        out_shape=jax.ShapeDtypeStruct((gy * gz, f5), BF),
        in_specs=[VMEM] * 2,
        out_specs=VMEM,
        compiler_params=PARAMS,
        name="add_planes",
    )(own, swap(other, 4))
    return features.reshape(1, gy, gz, f5)


def body(volume, conv4_weight, conv5_weight):
    paired = all(lax.axis_size(axis) == 2 for axis in GROUP)
    if paired and volume.shape[0] == 2 and volume.shape[1] == volume.shape[2] and conv4_weight.shape[4] == 2 * conv4_weight.shape[3]:
        return pair_body(volume, conv4_weight, conv5_weight)
    return general_body(volume, conv4_weight, conv5_weight)


def solution(mesh):
    return jax.shard_map(
        body,
        mesh=mesh,
        in_specs=(
            P(("sample", "gx"), "gy", "gz", None),
            P(),
            P(None, None, None, None, ("gy", "gz")),
        ),
        out_specs=P(("sample", "gx"), None, None, ("gy", "gz")),
        check_vma=False,
    )
```

```python
import functools

import jax
import jax.numpy as jnp
from jax import lax
from jax.experimental import pallas as pl
from jax.experimental.pallas import tpu as pltpu
from jax.sharding import PartitionSpec as P

BF = jnp.bfloat16
F32 = jnp.float32
VMEM = pl.BlockSpec(memory_space=pltpu.VMEM)
HBM = pl.BlockSpec(memory_space=pltpu.HBM)
GROUP = ("gx", "gy", "gz")
PARAMS = pltpu.CompilerParams(vmem_limit_bytes=8 * 2**20)


def extended(cells, sides, width):
    for axis, dim in sides:
        count = lax.axis_size(axis)
        ends = count - 1
        head = lax.slice_in_dim(cells, 0, width, axis=dim)
        tail = lax.slice_in_dim(cells, cells.shape[dim] - width, cells.shape[dim], axis=dim)
        cells = jnp.concatenate(
            [
                lax.ppermute(tail, axis, [(i, (i + 1) % count) for i in range(ends)]),
                cells,
                lax.ppermute(head, axis, [((i + 1) % count, i) for i in range(ends)]),
            ],
            axis=dim,
        )
    return cells


def conv_local(padded, kernel):
    extent_x = padded.shape[0] - 2
    extent_y = padded.shape[1] - 2
    extent_z = padded.shape[2] - 2
    inputs = padded.shape[3]
    summed = None
    for along_x in range(3):
        for along_y in range(3):
            for along_z in range(3):
                window = padded[
                    along_x : along_x + extent_x,
                    along_y : along_y + extent_y,
                    along_z : along_z + extent_z,
                ]
                window = window.reshape(extent_x * extent_y * extent_z, inputs)
                contrib = jnp.dot(
                    window, kernel[along_x, along_y, along_z], preferred_element_type=jnp.float32
                )
                summed = contrib if summed is None else summed + contrib
    return summed.reshape(extent_x, extent_y, extent_z, kernel.shape[4])


def pool_leaky(hidden):
    leaked = jnp.where(hidden > 0, hidden, 0.3 * hidden)
    sizes = leaked.shape
    blocks = leaked.reshape(sizes[0] // 2, 2, sizes[1] // 2, 2, sizes[2] // 2, 2, sizes[3])
    return jnp.max(blocks, axis=(1, 3, 5)).astype(jnp.bfloat16)


def general_body(volume, conv4_weight, conv5_weight):
    padded = extended(volume, (("gx", 0), ("gy", 1), ("gz", 2)), 1)
    pooled = pool_leaky(conv_local(padded, conv4_weight))
    strips = lax.all_gather(pooled, "gz", axis=2, tiled=True)
    slab = lax.all_gather(strips, "gy", axis=1, tiled=True)
    bordered = extended(slab, (("gx", 0),), 1)
    bordered = jnp.pad(bordered, ((0, 0), (1, 1), (1, 1), (0, 0)))
    return conv_local(bordered, conv5_weight).astype(jnp.bfloat16)


def leaky(v):
    return jnp.where(v > 0, v, 0.3 * v)


def shifted_copies(plane, out_ref, index, border):
    ny, nz, nc = plane.shape
    flat = plane.reshape(ny * nz, nc).astype(F32)
    at = lax.broadcasted_iota(jnp.int32, flat.shape, 0) % nz
    after = jnp.where(at == 0, 0.0, pltpu.roll(flat, 1, 0))
    before = jnp.where(at == nz - 1, 0.0, pltpu.roll(flat, ny * nz - 1, 0))
    for dz, moved in enumerate((after, flat, before)):
        if border:
            out_ref[dz, index, 0:border] = jnp.zeros((border, nz, nc), BF)
            out_ref[dz, index, border + ny : 2 * border + ny] = jnp.zeros((border, nz, nc), BF)
        out_ref[dz, index, border : border + ny] = moved.astype(BF).reshape(ny, nz, nc)


def windows(shift_ref, index, first, count):
    nz, nc = shift_ref.shape[3:]
    parts = []
    for dy in range(3):
        for dz in range(3):
            parts.append(shift_ref[dz, index, first + dy : first + dy + count].reshape(count * nz, nc))
    return jnp.concatenate(parts, axis=1)


def edge_columns(plane, flat_ref, at_z):
    ny, nz, nc = plane.shape
    flat_ref[...] = plane.reshape(ny * nz, nc).astype(F32)
    low = [flat_ref[pl.ds(z, ny, nz), :] for z in (0, 1)]
    high = [flat_ref[pl.ds(z, ny, nz), :] for z in (nz - 2, nz - 1)]
    return jnp.where(at_z == 0, jnp.concatenate(high, axis=1), jnp.concatenate(low, axis=1)).astype(BF)


def prepare_kernel(v_hbm, w_hbm, shift_ref, column_ref, sum_ref, w_ref, v_ref, flat_ref, v_sem, w_sem):
    load_v = pltpu.make_async_copy(v_hbm, v_ref, v_sem)
    loads = [pltpu.make_async_copy(w_hbm.at[dx], w_ref.at[dx], w_sem.at[dx]) for dx in range(3)]
    load_v.start()
    loads[1].start()
    loads[0].start(priority=1)
    loads[2].start(priority=1)
    planes, ny, nz, nc = v_ref.shape
    at_z = lax.axis_index("gz")
    load_v.wait()
    for p in range(v_ref.shape[0]):
        shifted_copies(v_ref[p], shift_ref, p, 1)
        column_ref[p] = edge_columns(v_ref[p], flat_ref, at_z)
    loads[1].wait()
    step = ny // 2
    for p in range(planes):
        for first in range(0, ny, step):
            begin = (p * ny + first) * nz
            rhs = w_ref[1].reshape(9 * nc, w_ref.shape[4])
            sums = jnp.dot(windows(shift_ref, p, first, step), rhs, preferred_element_type=F32)
            sum_ref[begin : begin + step * nz] = sums
    loads[0].wait()
    loads[2].wait()


def pack_kernel(r_ref, w_ref, own_ref, column_ref, sum_ref, out_ref, h_ref, shift_ref, flat_ref, pair_ref):
    at_x, at_y, at_z = (lax.axis_index(axis) for axis in GROUP)
    planes, ny, nz, nc = r_ref.shape
    filters = w_ref.shape[4]
    rows = ny * nz
    plane = r_ref[at_x]
    mine = 1 - at_x
    shifted_copies(plane, shift_ref, 0, 1)
    cells = ny * nz // 4
    columns = cells + (planes + 1) * nz
    first_row = (ny - 2) * (1 - at_y) + 1

    def put_edges(slot, source_ref, index, column):
        begin = pl.multiple_of(cells + slot * nz, 16)
        near = [source_ref[1, index, first_row + side] for side in range(2)]
        out_ref[pl.ds(begin, nz)] = jnp.concatenate(near, axis=1)
        begin = pl.multiple_of(columns + slot * ny, 16)
        out_ref[pl.ds(begin, ny)] = column

    put_edges(2 * mine, shift_ref, 0, edge_columns(plane, flat_ref, at_z))
    for p in range(planes):
        put_edges(at_x + p, own_ref, p, column_ref[p])
    step = 16
    for first in range(0, ny, step):
        count = step * nz
        near = w_ref[2 * mine].reshape(9 * nc, filters)
        far = w_ref[2 * at_x].reshape(9 * nc, filters)
        inner = sum_ref[pl.ds(pl.multiple_of(mine * rows + first * nz, 8), count)]
        inner += jnp.dot(windows(shift_ref, 0, first, step), near, preferred_element_type=F32)
        inner += jnp.dot(windows(own_ref, at_x, first, step), far, preferred_element_type=F32)
        outer = sum_ref[pl.ds(pl.multiple_of(at_x * rows + first * nz, 8), count)]
        outer += jnp.dot(windows(own_ref, mine, first, step), near, preferred_element_type=F32)
        h_ref[first * nz : first * nz + count] = jnp.maximum(inner, outer)

    def row(y):
        return h_ref[y * nz : (y + 1) * nz]

    low = -jnp.inf
    is_edge = lax.broadcasted_iota(jnp.int32, (nz, filters), 0) == (nz - 1) * (1 - at_z)
    for k in range(ny // 2):
        first, second = row(2 * k), row(2 * k + 1)
        if k == 0:
            first = jnp.where(at_y == 1, low, first)
        if k == ny // 2 - 1:
            second = jnp.where(at_y == 0, low, second)
        both = jnp.where(is_edge, low, jnp.maximum(first, second))
        for half in range(filters // 128):
            pair_ref[half, k * nz : (k + 1) * nz] = both[:, half * 128 : (half + 1) * 128]
    pooled = [
        jnp.maximum(pair_ref[half, pl.ds(0, cells, 2), :], pair_ref[half, pl.ds(1, cells, 2), :])
        for half in range(filters // 128)
    ]
    out_ref[0:cells] = leaky(jnp.concatenate(pooled, axis=1)).astype(out_ref.dtype)


def finish_kernel(
    q0, q1, q2, q3, w4_ref, w_ref, own_ref, other_ref, pack_ref, cross_ref, h_ref, full_ref, pair_ref, shift_ref, *, ny, nz, planes
):
    at_x, at_y, at_z = (lax.axis_index(axis) for axis in GROUP)
    mine = 1 - at_x
    filters = w_ref.shape[3]
    outs = w_ref.shape[4]
    nc = w4_ref.shape[3]
    here = 2 * at_y + at_z
    pack_ref[here] = q0[...]
    pack_ref[2 * (1 - at_y) + at_z] = q1[...]
    pack_ref[2 * at_y + 1 - at_z] = q2[...]
    pack_ref[2 * (1 - at_y) + 1 - at_z] = q3[...]
    py, pz = ny // 2, nz // 2
    cells = py * pz
    columns = cells + (planes + 1) * nz

    for slot in range(planes + 1):
        lines = []
        for side in range(4):
            lanes = slice(side % 2 * nc, side % 2 * nc + nc)
            begin = cells + slot * nz
            parts = [pack_ref[2 * (side // 2) + qz, begin : begin + nz, lanes] for qz in range(2)]
            lines.append(jnp.concatenate(parts, axis=0)[None])
        shifted_copies(jnp.concatenate(lines, axis=0), cross_ref.at[0], slot, 0)
        lines = []
        for side in range(4):
            lanes = slice(side % 2 * nc, side % 2 * nc + nc)
            begin = columns + slot * ny
            parts = [pack_ref[2 * qy + side // 2, begin : begin + ny, lanes] for qy in range(2)]
            lines.append(jnp.concatenate(parts, axis=0)[None])
        shifted_copies(jnp.concatenate(lines, axis=0), cross_ref.at[1], slot, 0)

    def cross_windows(kind, slot):
        parts = []
        for dy in range(3):
            for dz in range(3):
                along, over = (dz, dy) if kind == 0 else (dy, dz)
                part = cross_ref[kind, along, slot, over : over + 2]
                parts.append(part.reshape(part.shape[0] * part.shape[1], nc))
        return jnp.concatenate(parts, axis=1)

    wins = [jnp.concatenate([cross_windows(kind, slot) for kind in range(2)], axis=0) for slot in range(planes + 1)]
    rhs = w4_ref[...].reshape((planes + 1) * 9 * nc, filters)
    inner = jnp.dot(jnp.concatenate(wins, axis=1), rhs, preferred_element_type=F32)
    wins = [
        jnp.concatenate([cross_windows(kind, at_x + p) for kind in range(2)], axis=0) for p in range(planes)
    ]
    rhs = w4_ref[pl.ds(mine, planes)].reshape(planes * 9 * nc, filters)
    h_ref[...] = jnp.maximum(inner, jnp.dot(jnp.concatenate(wins, axis=1), rhs, preferred_element_type=F32))

    def halve(v, slot):
        parts = []
        for half in range(filters // 128):
            pair_ref[slot, half] = v[:, half * 128 : (half + 1) * 128]
            count = v.shape[0] // 2
            parts.append(
                jnp.maximum(pair_ref[slot, half, pl.ds(0, count, 2), :], pair_ref[slot, half, pl.ds(1, count, 2), :])
            )
        return jnp.concatenate(parts, axis=1)

    for qy in range(2):
        for qz in range(2):
            pooled = pack_ref[2 * qy + qz, 0:cells].astype(F32)
            full_ref[qy * py : (qy + 1) * py, qz * pz : (qz + 1) * pz] = pooled.reshape(py, pz, filters)
    pooled = full_ref[...]
    at_row = lax.broadcasted_iota(jnp.int32, (2 * py, 1, filters), 0)
    at_col = lax.broadcasted_iota(jnp.int32, (1, 2 * pz, filters), 1)
    for side in range(2):
        first = side * 2 * nz
        line = h_ref[first : first + 2 * nz]
        line = leaky(halve(line, side))
        pooled = jnp.maximum(pooled, jnp.where(at_row == py - 1 + side, line[None], -jnp.inf))
        first = 4 * nz + side * 2 * ny
        line = h_ref[first : first + 2 * ny]
        line = leaky(halve(line, 2 + side))
        pooled = jnp.maximum(pooled, jnp.where(at_col == pz - 1 + side, line[:, None, :], -jnp.inf))
    shifted_copies(pooled.astype(BF), shift_ref, 0, 1)
    rhs = jnp.concatenate(
        [w_ref[1].reshape(9 * filters, outs), w_ref[2 * at_x].reshape(9 * filters, outs)], axis=1
    )
    step = 8
    for first in range(0, ny, step):
        sums = jnp.dot(windows(shift_ref, 0, first, step), rhs, preferred_element_type=F32)
        own_ref[first * nz : (first + step) * nz] = sums[:, :outs]
        other_ref[first * nz : (first + step) * nz] = sums[:, outs:].astype(other_ref.dtype)


def add_kernel(own_ref, other_ref, out_ref):
    out_ref[...] = (own_ref[...] + other_ref[...]).astype(out_ref.dtype)


def pair_body(volume, conv4_weight, conv5_weight):
    planes, ny, nz, nc = volume.shape
    f4, f5 = conv4_weight.shape[4], conv5_weight.shape[4]

    def swap(x, flips):
        return lax.ppermute(x, GROUP, [(i, i ^ flips) for i in range(8)])

    cost = functools.partial(pl.CostEstimate, transcendentals=0)
    rows = ny * nz
    theirs = swap(volume, 4)
    moved, columns, sums, kernel4 = pl.pallas_call(
        prepare_kernel,
        out_shape=(
            jax.ShapeDtypeStruct((3, planes, ny + 2, nz, nc), BF),
            jax.ShapeDtypeStruct((planes, ny, 2 * nc), BF),
            jax.ShapeDtypeStruct((planes * rows, f4), F32),
            jax.ShapeDtypeStruct(conv4_weight.shape, BF),
        ),
        in_specs=[HBM, HBM],
        out_specs=(VMEM,) * 4,
        scratch_shapes=[
            pltpu.VMEM(volume.shape, BF),
            pltpu.VMEM((rows, nc), F32),
            pltpu.SemaphoreType.DMA,
            pltpu.SemaphoreType.DMA((3,)),
        ],
        cost_estimate=cost(flops=20 * planes * rows * nc, bytes_accessed=54 * nc * f4),
        compiler_params=PARAMS,
        name="prepare",
    )(*(pltpu.with_memory_space_constraint(x, pltpu.HBM) for x in (volume, conv4_weight)))
    packed = rows // 4 + (planes + 1) * (ny + nz)
    pack = pl.pallas_call(
        pack_kernel,
        out_shape=jax.ShapeDtypeStruct((packed, f4), BF),
        in_specs=[VMEM] * 5,
        out_specs=VMEM,
        scratch_shapes=[
            pltpu.VMEM((rows, f4), F32),
            pltpu.VMEM((3, 1, ny + 2, nz, nc), BF),
            pltpu.VMEM((rows, nc), F32),
            pltpu.VMEM((f4 // 128, rows // 2, 128), F32),
        ],
        cost_estimate=cost(flops=3 * 2 * rows * 9 * nc * f4, bytes_accessed=54 * nc * f4),
        compiler_params=PARAMS,
        name="conv4_pool_pack",
    )(theirs, kernel4, moved, columns, sums)
    by_y = swap(pack, 2)
    by_z = swap(pack, 1)
    by_both = swap(pack, 3)
    gy, gz = 2 * ny // 2, 2 * nz // 2
    own, other = pl.pallas_call(
        functools.partial(finish_kernel, ny=ny, nz=nz, planes=planes),
        out_shape=(jax.ShapeDtypeStruct((gy * gz, f5), F32), jax.ShapeDtypeStruct((gy * gz, f5), BF)),
        in_specs=[VMEM] * 6,
        out_specs=(VMEM, VMEM),
        scratch_shapes=[
            pltpu.VMEM((4, packed, f4), BF),
            pltpu.VMEM((2, 3, planes + 1, 4, 2 * nz, nc), BF),
            pltpu.VMEM((4 * ny + 4 * nz, f4), F32),
            pltpu.VMEM((gy, gz, f4), F32),
            pltpu.VMEM((4, f4 // 128, 2 * nz, 128), F32),
            pltpu.VMEM((3, 1, gy + 2, gz, f4), BF),
        ],
        cost_estimate=cost(flops=4 * gy * gz * 9 * f4 * f5, bytes_accessed=36 * f4 * f5),
        compiler_params=PARAMS,
        name="finish_and_conv5",
    )(pack, by_y, by_z, by_both, kernel4, conv5_weight)
    features = pl.pallas_call(
        add_kernel,
        out_shape=jax.ShapeDtypeStruct((gy * gz, f5), BF),
        in_specs=[VMEM] * 2,
        out_specs=VMEM,
        compiler_params=PARAMS,
        name="add_planes",
    )(own, swap(other, 4))
    return features.reshape(1, gy, gz, f5)


def body(volume, conv4_weight, conv5_weight):
    paired = all(lax.axis_size(axis) == 2 for axis in GROUP)
    if paired and volume.shape[0] == 2 and volume.shape[1] == volume.shape[2] and conv4_weight.shape[4] == 2 * conv4_weight.shape[3]:
        return pair_body(volume, conv4_weight, conv5_weight)
    return general_body(volume, conv4_weight, conv5_weight)


def solution(mesh):
    return jax.shard_map(
        body,
        mesh=mesh,
        in_specs=(
            P(("sample", "gx"), "gy", "gz", None),
            P(),
            P(None, None, None, None, ("gy", "gz")),
        ),
        out_specs=P(("sample", "gx"), None, None, ("gy", "gz")),
        check_vma=False,
    )
```

```python
import functools

import jax
import jax.numpy as jnp
from jax import lax
from jax.experimental import pallas as pl
from jax.experimental.pallas import tpu as pltpu
from jax.sharding import PartitionSpec as P

BF = jnp.bfloat16
F32 = jnp.float32
VMEM = pl.BlockSpec(memory_space=pltpu.VMEM)
HBM = pl.BlockSpec(memory_space=pltpu.HBM)
GROUP = ("gx", "gy", "gz")
PARAMS = pltpu.CompilerParams(vmem_limit_bytes=8 * 2**20)


def extended(cells, sides, width):
    for axis, dim in sides:
        count = lax.axis_size(axis)
        ends = count - 1
        head = lax.slice_in_dim(cells, 0, width, axis=dim)
        tail = lax.slice_in_dim(cells, cells.shape[dim] - width, cells.shape[dim], axis=dim)
        cells = jnp.concatenate(
            [
                lax.ppermute(tail, axis, [(i, (i + 1) % count) for i in range(ends)]),
                cells,
                lax.ppermute(head, axis, [((i + 1) % count, i) for i in range(ends)]),
            ],
            axis=dim,
        )
    return cells


def conv_local(padded, kernel):
    extent_x = padded.shape[0] - 2
    extent_y = padded.shape[1] - 2
    extent_z = padded.shape[2] - 2
    inputs = padded.shape[3]
    summed = None
    for along_x in range(3):
        for along_y in range(3):
            for along_z in range(3):
                window = padded[
                    along_x : along_x + extent_x,
                    along_y : along_y + extent_y,
                    along_z : along_z + extent_z,
                ]
                window = window.reshape(extent_x * extent_y * extent_z, inputs)
                contrib = jnp.dot(
                    window, kernel[along_x, along_y, along_z], preferred_element_type=jnp.float32
                )
                summed = contrib if summed is None else summed + contrib
    return summed.reshape(extent_x, extent_y, extent_z, kernel.shape[4])


def pool_leaky(hidden):
    leaked = jnp.where(hidden > 0, hidden, 0.3 * hidden)
    sizes = leaked.shape
    blocks = leaked.reshape(sizes[0] // 2, 2, sizes[1] // 2, 2, sizes[2] // 2, 2, sizes[3])
    return jnp.max(blocks, axis=(1, 3, 5)).astype(jnp.bfloat16)


def general_body(volume, conv4_weight, conv5_weight):
    padded = extended(volume, (("gx", 0), ("gy", 1), ("gz", 2)), 1)
    pooled = pool_leaky(conv_local(padded, conv4_weight))
    strips = lax.all_gather(pooled, "gz", axis=2, tiled=True)
    slab = lax.all_gather(strips, "gy", axis=1, tiled=True)
    bordered = extended(slab, (("gx", 0),), 1)
    bordered = jnp.pad(bordered, ((0, 0), (1, 1), (1, 1), (0, 0)))
    return conv_local(bordered, conv5_weight).astype(jnp.bfloat16)


def leaky(v):
    return jnp.where(v > 0, v, 0.3 * v)


def shifted_copies(plane, out_ref, index, border):
    ny, nz, nc = plane.shape
    flat = plane.reshape(ny * nz, nc).astype(F32)
    at = lax.broadcasted_iota(jnp.int32, flat.shape, 0) % nz
    after = jnp.where(at == 0, 0.0, pltpu.roll(flat, 1, 0))
    before = jnp.where(at == nz - 1, 0.0, pltpu.roll(flat, ny * nz - 1, 0))
    for dz, moved in enumerate((after, flat, before)):
        if border:
            out_ref[dz, index, 0:border] = jnp.zeros((border, nz, nc), BF)
            out_ref[dz, index, border + ny : 2 * border + ny] = jnp.zeros((border, nz, nc), BF)
        out_ref[dz, index, border : border + ny] = moved.astype(BF).reshape(ny, nz, nc)


def windows(shift_ref, index, first, count):
    nz, nc = shift_ref.shape[3:]
    parts = []
    for dy in range(3):
        for dz in range(3):
            parts.append(shift_ref[dz, index, first + dy : first + dy + count].reshape(count * nz, nc))
    return jnp.concatenate(parts, axis=1)


def edge_columns(plane, flat_ref, at_z):
    ny, nz, nc = plane.shape
    flat_ref[...] = plane.reshape(ny * nz, nc).astype(F32)
    low = [flat_ref[pl.ds(z, ny, nz), :] for z in (0, 1)]
    high = [flat_ref[pl.ds(z, ny, nz), :] for z in (nz - 2, nz - 1)]
    return jnp.where(at_z == 0, jnp.concatenate(high, axis=1), jnp.concatenate(low, axis=1)).astype(BF)


def prepare_kernel(v_hbm, w_hbm, shift_ref, column_ref, sum_ref, w_ref, v_ref, flat_ref, v_sem, w_sem):
    load_v = pltpu.make_async_copy(v_hbm, v_ref, v_sem)
    loads = [pltpu.make_async_copy(w_hbm.at[dx], w_ref.at[dx], w_sem.at[dx]) for dx in range(3)]
    load_v.start()
    loads[1].start()
    loads[0].start(priority=1)
    loads[2].start(priority=1)
    planes, ny, nz, nc = v_ref.shape
    at_z = lax.axis_index("gz")
    load_v.wait()
    for p in range(v_ref.shape[0]):
        shifted_copies(v_ref[p], shift_ref, p, 1)
        column_ref[p] = edge_columns(v_ref[p], flat_ref, at_z)
    loads[1].wait()
    step = ny // 2
    for p in range(planes):
        for first in range(0, ny, step):
            begin = (p * ny + first) * nz
            rhs = w_ref[1].reshape(9 * nc, w_ref.shape[4])
            sums = jnp.dot(windows(shift_ref, p, first, step), rhs, preferred_element_type=F32)
            sum_ref[begin : begin + step * nz] = sums
    loads[0].wait()
    loads[2].wait()


def pack_kernel(r_ref, w_ref, own_ref, column_ref, sum_ref, out_ref, h_ref, shift_ref, flat_ref, pair_ref):
    at_x, at_y, at_z = (lax.axis_index(axis) for axis in GROUP)
    planes, ny, nz, nc = r_ref.shape
    filters = w_ref.shape[4]
    rows = ny * nz
    plane = r_ref[at_x]
    mine = 1 - at_x
    shifted_copies(plane, shift_ref, 0, 1)
    cells = ny * nz // 4
    columns = cells + (planes + 1) * nz
    first_row = (ny - 2) * (1 - at_y) + 1

    def put_edges(slot, source_ref, index, column):
        begin = pl.multiple_of(cells + slot * nz, 16)
        near = [source_ref[1, index, first_row + side] for side in range(2)]
        out_ref[pl.ds(begin, nz)] = jnp.concatenate(near, axis=1)
        begin = pl.multiple_of(columns + slot * ny, 16)
        out_ref[pl.ds(begin, ny)] = column

    put_edges(2 * mine, shift_ref, 0, edge_columns(plane, flat_ref, at_z))
    for p in range(planes):
        put_edges(at_x + p, own_ref, p, column_ref[p])
    step = 16
    for first in range(0, ny, step):
        count = step * nz
        near = w_ref[2 * mine].reshape(9 * nc, filters)
        far = w_ref[2 * at_x].reshape(9 * nc, filters)
        inner = sum_ref[pl.ds(pl.multiple_of(mine * rows + first * nz, 8), count)]
        inner += jnp.dot(windows(shift_ref, 0, first, step), near, preferred_element_type=F32)
        inner += jnp.dot(windows(own_ref, at_x, first, step), far, preferred_element_type=F32)
        outer = sum_ref[pl.ds(pl.multiple_of(at_x * rows + first * nz, 8), count)]
        outer += jnp.dot(windows(own_ref, mine, first, step), near, preferred_element_type=F32)
        h_ref[first * nz : first * nz + count] = jnp.maximum(inner, outer)

    def row(y):
        return h_ref[y * nz : (y + 1) * nz]

    low = -jnp.inf
    is_edge = lax.broadcasted_iota(jnp.int32, (nz, filters), 0) == (nz - 1) * (1 - at_z)
    for k in range(ny // 2):
        first, second = row(2 * k), row(2 * k + 1)
        if k == 0:
            first = jnp.where(at_y == 1, low, first)
        if k == ny // 2 - 1:
            second = jnp.where(at_y == 0, low, second)
        both = jnp.where(is_edge, low, jnp.maximum(first, second))
        for half in range(filters // 128):
            pair_ref[half, k * nz : (k + 1) * nz] = both[:, half * 128 : (half + 1) * 128]
    pooled = [
        jnp.maximum(pair_ref[half, pl.ds(0, cells, 2), :], pair_ref[half, pl.ds(1, cells, 2), :])
        for half in range(filters // 128)
    ]
    out_ref[0:cells] = leaky(jnp.concatenate(pooled, axis=1)).astype(out_ref.dtype)


def finish_kernel(
    q0, q1, q2, q3, w4_ref, w_ref, own_ref, other_ref, pack_ref, cross_ref, h_ref, full_ref, pair_ref, shift_ref, *, ny, nz, planes
):
    at_x, at_y, at_z = (lax.axis_index(axis) for axis in GROUP)
    mine = 1 - at_x
    filters = w_ref.shape[3]
    outs = w_ref.shape[4]
    nc = w4_ref.shape[3]
    here = 2 * at_y + at_z
    pack_ref[here] = q0[...]
    pack_ref[2 * (1 - at_y) + at_z] = q1[...]
    pack_ref[2 * at_y + 1 - at_z] = q2[...]
    pack_ref[2 * (1 - at_y) + 1 - at_z] = q3[...]
    py, pz = ny // 2, nz // 2
    cells = py * pz
    columns = cells + (planes + 1) * nz

    for slot in range(planes + 1):
        lines = []
        for side in range(4):
            lanes = slice(side % 2 * nc, side % 2 * nc + nc)
            begin = cells + slot * nz
            parts = [pack_ref[2 * (side // 2) + qz, begin : begin + nz, lanes] for qz in range(2)]
            lines.append(jnp.concatenate(parts, axis=0)[None])
        shifted_copies(jnp.concatenate(lines, axis=0), cross_ref.at[0], slot, 0)
        lines = []
        for side in range(4):
            lanes = slice(side % 2 * nc, side % 2 * nc + nc)
            begin = columns + slot * ny
            parts = [pack_ref[2 * qy + side // 2, begin : begin + ny, lanes] for qy in range(2)]
            lines.append(jnp.concatenate(parts, axis=0)[None])
        shifted_copies(jnp.concatenate(lines, axis=0), cross_ref.at[1], slot, 0)

    def cross_windows(kind, slot):
        parts = []
        for dy in range(3):
            for dz in range(3):
                along, over = (dz, dy) if kind == 0 else (dy, dz)
                part = cross_ref[kind, along, slot, over : over + 2]
                parts.append(part.reshape(part.shape[0] * part.shape[1], nc))
        return jnp.concatenate(parts, axis=1)

    wins = [jnp.concatenate([cross_windows(kind, slot) for kind in range(2)], axis=0) for slot in range(planes + 1)]
    rhs = w4_ref[...].reshape((planes + 1) * 9 * nc, filters)
    inner = jnp.dot(jnp.concatenate(wins, axis=1), rhs, preferred_element_type=F32)
    wins = [
        jnp.concatenate([cross_windows(kind, at_x + p) for kind in range(2)], axis=0) for p in range(planes)
    ]
    rhs = w4_ref[pl.ds(mine, planes)].reshape(planes * 9 * nc, filters)
    h_ref[...] = jnp.maximum(inner, jnp.dot(jnp.concatenate(wins, axis=1), rhs, preferred_element_type=F32))

    def halve(v, slot):
        parts = []
        for half in range(filters // 128):
            pair_ref[slot, half] = v[:, half * 128 : (half + 1) * 128]
            count = v.shape[0] // 2
            parts.append(
                jnp.maximum(pair_ref[slot, half, pl.ds(0, count, 2), :], pair_ref[slot, half, pl.ds(1, count, 2), :])
            )
        return jnp.concatenate(parts, axis=1)

    for qy in range(2):
        for qz in range(2):
            pooled = pack_ref[2 * qy + qz, 0:cells].astype(F32)
            full_ref[qy * py : (qy + 1) * py, qz * pz : (qz + 1) * pz] = pooled.reshape(py, pz, filters)
    pooled = full_ref[...]
    at_row = lax.broadcasted_iota(jnp.int32, (2 * py, 1, filters), 0)
    at_col = lax.broadcasted_iota(jnp.int32, (1, 2 * pz, filters), 1)
    for side in range(2):
        first = side * 2 * nz
        line = h_ref[first : first + 2 * nz]
        line = leaky(halve(line, side))
        pooled = jnp.maximum(pooled, jnp.where(at_row == py - 1 + side, line[None], -jnp.inf))
        first = 4 * nz + side * 2 * ny
        line = h_ref[first : first + 2 * ny]
        line = leaky(halve(line, 2 + side))
        pooled = jnp.maximum(pooled, jnp.where(at_col == pz - 1 + side, line[:, None, :], -jnp.inf))
    shifted_copies(pooled.astype(BF), shift_ref, 0, 1)
    rhs = jnp.concatenate(
        [w_ref[1].reshape(9 * filters, outs), w_ref[2 * at_x].reshape(9 * filters, outs)], axis=1
    )
    step = 8
    for first in range(0, ny, step):
        sums = jnp.dot(windows(shift_ref, 0, first, step), rhs, preferred_element_type=F32)
        own_ref[first * nz : (first + step) * nz] = sums[:, :outs]
        other_ref[first * nz : (first + step) * nz] = sums[:, outs:].astype(other_ref.dtype)


def add_kernel(own_ref, other_ref, out_ref):
    out_ref[...] = (own_ref[...] + other_ref[...]).astype(out_ref.dtype)


def pair_body(volume, conv4_weight, conv5_weight):
    planes, ny, nz, nc = volume.shape
    f4, f5 = conv4_weight.shape[4], conv5_weight.shape[4]

    def swap(x, flips):
        return lax.ppermute(x, GROUP, [(i, i ^ flips) for i in range(lax.axis_size(GROUP))])

    cost = functools.partial(pl.CostEstimate, transcendentals=0)
    rows = ny * nz
    theirs = swap(volume, 4)
    moved, columns, sums, kernel4 = pl.pallas_call(
        prepare_kernel,
        out_shape=(
            jax.ShapeDtypeStruct((3, planes, ny + 2, nz, nc), BF),
            jax.ShapeDtypeStruct((planes, ny, 2 * nc), BF),
            jax.ShapeDtypeStruct((planes * rows, f4), F32),
            jax.ShapeDtypeStruct(conv4_weight.shape, BF),
        ),
        in_specs=[HBM, HBM],
        out_specs=(VMEM,) * 4,
        scratch_shapes=[
            pltpu.VMEM(volume.shape, BF),
            pltpu.VMEM((rows, nc), F32),
            pltpu.SemaphoreType.DMA,
            pltpu.SemaphoreType.DMA((3,)),
        ],
        cost_estimate=cost(flops=20 * planes * rows * nc, bytes_accessed=54 * nc * f4),
        compiler_params=PARAMS,
        name="prepare",
    )(*(pltpu.with_memory_space_constraint(x, pltpu.HBM) for x in (volume, conv4_weight)))
    packed = rows // 4 + (planes + 1) * (ny + nz)
    pack = pl.pallas_call(
        pack_kernel,
        out_shape=jax.ShapeDtypeStruct((packed, f4), BF),
        in_specs=[VMEM] * 5,
        out_specs=VMEM,
        scratch_shapes=[
            pltpu.VMEM((rows, f4), F32),
            pltpu.VMEM((3, 1, ny + 2, nz, nc), BF),
            pltpu.VMEM((rows, nc), F32),
            pltpu.VMEM((f4 // 128, rows // 2, 128), F32),
        ],
        cost_estimate=cost(flops=3 * 2 * rows * 9 * nc * f4, bytes_accessed=54 * nc * f4),
        compiler_params=PARAMS,
        name="conv4_pool_pack",
    )(theirs, kernel4, moved, columns, sums)
    by_y = swap(pack, 2)
    by_z = swap(pack, 1)
    by_both = swap(pack, 3)
    gy, gz = 2 * ny // 2, 2 * nz // 2
    own, other = pl.pallas_call(
        functools.partial(finish_kernel, ny=ny, nz=nz, planes=planes),
        out_shape=(jax.ShapeDtypeStruct((gy * gz, f5), F32), jax.ShapeDtypeStruct((gy * gz, f5), BF)),
        in_specs=[VMEM] * 6,
        out_specs=(VMEM, VMEM),
        scratch_shapes=[
            pltpu.VMEM((4, packed, f4), BF),
            pltpu.VMEM((2, 3, planes + 1, 4, 2 * nz, nc), BF),
            pltpu.VMEM((4 * ny + 4 * nz, f4), F32),
            pltpu.VMEM((gy, gz, f4), F32),
            pltpu.VMEM((4, f4 // 128, 2 * nz, 128), F32),
            pltpu.VMEM((3, 1, gy + 2, gz, f4), BF),
        ],
        cost_estimate=cost(flops=4 * gy * gz * 9 * f4 * f5, bytes_accessed=36 * f4 * f5),
        compiler_params=PARAMS,
        name="finish_and_conv5",
    )(pack, by_y, by_z, by_both, kernel4, conv5_weight)
    features = pl.pallas_call(
        add_kernel,
        out_shape=jax.ShapeDtypeStruct((gy * gz, f5), BF),
        in_specs=[VMEM] * 2,
        out_specs=VMEM,
        compiler_params=PARAMS,
        name="add_planes",
    )(own, swap(other, 4))
    return features.reshape(1, gy, gz, f5)


def body(volume, conv4_weight, conv5_weight):
    paired = all(lax.axis_size(axis) == 2 for axis in GROUP)
    if paired and volume.shape[0] == 2 and volume.shape[1] == volume.shape[2] and conv4_weight.shape[4] == 2 * conv4_weight.shape[3]:
        return pair_body(volume, conv4_weight, conv5_weight)
    return general_body(volume, conv4_weight, conv5_weight)


def solution(mesh):
    return jax.shard_map(
        body,
        mesh=mesh,
        in_specs=(
            P(("sample", "gx"), "gy", "gz", None),
            P(),
            P(None, None, None, None, ("gy", "gz")),
        ),
        out_specs=P(("sample", "gx"), None, None, ("gy", "gz")),
        check_vma=False,
    )
```
